128 devices in a mesh: seq: 16 (over y, z_hi, core), head: 8 (over z_lo, x).
Axes of the slice: x: 4, y: 4, z: 4 (z_hi: 2, z_lo: 2; z = z_hi * 2 + z_lo), core: 2. Of those that a mesh axis runs over, the one named last changes fastest.
Arguments:
- queries: bfloat16 [8192, 8192], P(('seq', 'head')), may hold values from -6 to 6
- new_keys: bfloat16 [8192, 1024], P(('seq', 'head')), may hold values from -6 to 6
- new_values: bfloat16 [8192, 1024], P(('seq', 'head')), may hold values from -6 to 6
- cache_keys: bfloat16 [4096, 1024], P('seq', 'head'), may hold values from -6 to 6
- cache_values: bfloat16 [4096, 1024], P('seq', 'head'), may hold values from -6 to 6
- retrieval: int32 [8], replicated, may hold values from 0 to 1, as said below
- sinks: int32 [8], replicated, may hold values from 32 to 64, as said below
- windows: int32 [8], replicated, may hold values from 768 to 1536, as said below
Outputs:
- attended: bfloat16 [8192, 8192], P(('seq', 'head'))
The draws below stay inside these ranges and needn't reach their ends.
Inputs may be any that keep to these rules, and one draw needn't show every extreme that they name: `retrieval`: exactly 2 of the 8 entries are 1, the others 0. `sinks`: the largest entry is exactly 64. `windows`: the largest entry is exactly 1536.
All inputs are finite; a program needn't handle non-finite values.
Results may differ from the reference program's by a relative error of at most 0.01.
Values may be sent and summed in bfloat16 or wider, within the bound.
No kernel may reach another device: no remote copies, remote signals or barrier semaphores. Data moves between devices by JAX's collectives and lax.ppermute only.
A program may use at most 448 MiB of HBM per device.

```python
import math
import jax
import jax.numpy as jnp
from jax import lax

HQ = 64
KVH = 8
DH = 128
RET = 2
SINK_MOST = 64
WIN_MOST = 1536
TOKENS = 8192
PREFIX = 4096


def draw_queries(key, part):
    key = jax.random.fold_in(key, 1)
    shape = (TOKENS, KVH, HQ // KVH, DH)
    filled = jnp.clip(jax.random.normal(key, shape, jnp.float32), -6.0, 6.0)
    return filled.reshape(TOKENS, HQ * DH).astype(jnp.bfloat16)


def draw_cache_keys(key, part):
    key = jax.random.fold_in(key, 2)
    shape = (PREFIX, KVH, DH)
    filled = jnp.clip(jax.random.normal(key, shape, jnp.float32), -6.0, 6.0)
    return filled.reshape(PREFIX, KVH * DH).astype(jnp.bfloat16)


def draw_retrieval(key, part):
    key = jax.random.fold_in(key, 3)
    order = jax.random.permutation(key, KVH)
    return (order < RET).astype(jnp.int32)


def draw_sinks(key, part):
    key = jax.random.fold_in(key, 4)
    first, second = jax.random.split(key)
    counts = jax.random.randint(first, (KVH,), SINK_MOST // 2, SINK_MOST + 1)
    spot = jax.random.randint(second, (), 0, KVH)
    return jnp.where(jnp.arange(KVH) == spot, SINK_MOST, counts).astype(jnp.int32)


def draw_windows(key, part):
    key = jax.random.fold_in(key, 5)
    first, second = jax.random.split(key)
    counts = jax.random.randint(first, (KVH,), WIN_MOST // 2, WIN_MOST + 1)
    spot = jax.random.randint(second, (), 0, KVH)
    return jnp.where(jnp.arange(KVH) == spot, WIN_MOST, counts).astype(jnp.int32)


def level_of(key, dims, pieces, low, high):
    loudness, own = 1.0, jax.random.fold_in(key, 6)
    for position, blocks in pieces:
        steps = jnp.exp(jax.random.uniform(jax.random.fold_in(own, position), (blocks,), jnp.float32, low / len(pieces), high / len(pieces)))
        loudness = loudness * jnp.repeat(steps, dims[position] // blocks).reshape([-1 if axis == position else 1 for axis in range(len(dims))])
    return loudness


def gaussian(rng, extent, scale, reach, pieces=(), held_as=jnp.bfloat16):
    factor_of = level_of(rng, extent, pieces, -0.22, 0.18) if pieces else 1.0
    entries = jax.random.normal(rng, extent, jnp.float32) * scale * factor_of
    return jnp.minimum(jnp.maximum(entries, -reach), reach).astype(held_as)


def setup_inputs(seed: int = 0) -> dict:
    arg_keys = jax.random.split(jax.random.key(seed), 9)
    return {
        "queries": draw_queries(jax.random.fold_in(arg_keys[8], 71), 0),
        "new_keys": gaussian(arg_keys[1], (TOKENS, KVH * DH), 1.0, 6.0, ((0, 128),)),
        "new_values": gaussian(arg_keys[2], (TOKENS, KVH * DH), 1.0, 6.0, ((0, 128),)),
        "cache_keys": draw_cache_keys(jax.random.fold_in(arg_keys[8], 71), 0),
        "cache_values": gaussian(arg_keys[4], (PREFIX, KVH * DH), 1.0, 6.0, ((0, 16), (1, 8))),
        "retrieval": draw_retrieval(jax.random.fold_in(arg_keys[8], 71), 0),
        "sinks": draw_sinks(jax.random.fold_in(arg_keys[8], 71), 0),
        "windows": draw_windows(jax.random.fold_in(arg_keys[8], 71), 0),
    }


def reference(queries, new_keys, new_values, cache_keys, cache_values, retrieval, sinks, windows):
    keys = jnp.concatenate([cache_keys, new_keys], 0)
    values = jnp.concatenate([cache_values, new_values], 0)
    group = HQ // KVH
    scale = 1.0 / math.sqrt(DH)
    key_pos = jnp.arange(PREFIX + TOKENS, dtype=jnp.int32)
    block = math.gcd(512, TOKENS)

    def one_head(g):
        key_rows = lax.dynamic_slice_in_dim(keys, (g * DH).astype(jnp.int32), DH, 1).astype(jnp.float32)
        value_rows = lax.dynamic_slice_in_dim(values, (g * DH).astype(jnp.int32), DH, 1).astype(jnp.float32)
        query_cols = lax.dynamic_slice_in_dim(queries, (g * group * DH).astype(jnp.int32), group * DH, 1)
        query_cols = query_cols.reshape(TOKENS, group, DH)
        flag = retrieval[g]
        sink = sinks[g]
        window = windows[g]

        def one_block(b):
            start = (b * block).astype(jnp.int32)
            query_block = lax.dynamic_slice_in_dim(query_cols, start, block, 0).astype(jnp.float32)
            query_pos = PREFIX + start + jnp.arange(block, dtype=jnp.int32)
            scores = jnp.einsum('tqd,kd->tqk', query_block, key_rows) * scale
            before = key_pos[None, :] <= query_pos[:, None]
            near = key_pos[None, :] > query_pos[:, None] - window
            visible = before & ((flag == 1) | (key_pos[None, :] < sink) | near)
            scores = jnp.where(visible[:, None, :], scores, -jnp.inf)
            top = lax.optimization_barrier(jnp.max(scores, -1))
            expo = jnp.exp(scores - top[..., None])
            total = lax.optimization_barrier(jnp.sum(expo, -1))
            weights = lax.optimization_barrier(expo.astype(jnp.bfloat16)).astype(jnp.float32)
            summed = jnp.einsum('tqk,kd->tqd', weights, value_rows)
            return (summed / total[..., None]).astype(jnp.bfloat16)
        result = lax.map(one_block, jnp.arange(TOKENS // block, dtype=jnp.int32))
        return result.reshape(TOKENS, group * DH)
    outputs = lax.map(one_head, jnp.arange(KVH, dtype=jnp.int32))
    return jnp.transpose(outputs, (1, 0, 2)).reshape(TOKENS, HQ * DH)
```

```python
import functools
import math

import jax
import jax.numpy as jnp
from jax import lax
from jax.experimental import pallas as pl
from jax.experimental.pallas import tpu as pltpu
from jax.sharding import PartitionSpec as P

HQ = 64
KVH = 8
DH = 128
GROUP = HQ // KVH
WIDE = GROUP * DH
SINKS = 64

SEQ, HEAD = 16, 8
TOK = 64
BLOCK = TOK * HEAD
PRE = 256
CARRY = BLOCK + SINKS
WINDOW_BLOCKS = 3

RING = 4
KEY_PARTS = 2
PIECE = TOK * RING
R_NEW_DEV = TOK // KEY_PARTS
R_NEW = BLOCK // KEY_PARTS
R_PRE = PRE // KEY_PARTS
R_SEND = R_NEW_DEV + R_PRE
R_ROWS = R_NEW + R_PRE
R_UNITS = 4
R_LANES = WIDE + DH

LOG2E_SCALED = math.log2(math.e) / math.sqrt(DH)
HIDDEN = -1e30
NT = (((1,), (1,)), ((), ()))

SMEM = pl.BlockSpec(memory_space=pltpu.SMEM)
bf16 = jnp.bfloat16
f32 = jnp.float32


VMEM = pl.BlockSpec(memory_space=pltpu.VMEM)


def call(kernel, outs, ins, flops=0, nbytes=2**20, scratch=(), vmem=44):
    def spec(a):
        if a.dtype == jnp.int32:
            return SMEM
        return VMEM if a.dtype == f32 else pl.BlockSpec(a.shape, lambda i: (0,) * len(a.shape))

    return pl.pallas_call(
        kernel,
        grid=(1,),
        out_shape=outs,
        in_specs=[spec(a) for a in ins],
        out_specs=jax.tree.map(spec, outs),
        scratch_shapes=list(scratch),
        compiler_params=pltpu.CompilerParams(vmem_limit_bytes=vmem * 2**20),
        cost_estimate=pl.CostEstimate(flops=flops, bytes_accessed=nbytes, transcendentals=0),
    )(*ins)


def retrieval_groups(flags):
    low = jnp.int32(0)
    high = jnp.int32(0)
    for g in range(KVH):
        high = jnp.where(flags[g] == 1, g, high)
        low = jnp.where(flags[KVH - 1 - g] == 1, KVH - 1 - g, low)
    return low, high


def pack_kv_kernel(flags, nk, nv, ck, cv, out, cache):
    groups = retrieval_groups(flags)
    cache[:, 0:DH] = ck[...]
    cache[:, DH:] = cv[...]
    for h in range(HEAD):
        out[h, 0:TOK, 0:DH] = nk[:, h * DH : (h + 1) * DH]
        out[h, 0:TOK, DH:] = nv[:, h * DH : (h + 1) * DH]
        x = h % RING
        cols = pl.ds(pl.multiple_of(groups[x // KEY_PARTS] * DH, DH), DH)
        part = x % KEY_PARTS
        rows = slice(part * R_NEW_DEV, (part + 1) * R_NEW_DEV)
        end = TOK + R_NEW_DEV
        out[h, TOK:end, 0:DH] = nk[rows, cols]
        out[h, TOK:end, DH:] = nv[rows, cols]
        rows = slice(part * R_PRE, (part + 1) * R_PRE)
        out[h, end:, 0:DH] = ck[rows, :]
        out[h, end:, DH:] = cv[rows, :]


def unpack_kv_kernel(flags, place, got, cache, first, second, third, part, own, two_on, odd_on):
    s = place[0]
    low, high = retrieval_groups(flags)
    source = jnp.where((place[1] % RING) // KEY_PARTS == 0, low, high)
    end = TOK + R_NEW_DEV
    part[0:R_PRE, :] = got[source, end:, :]
    part[R_PRE:, :] = got[:, TOK:end, :].reshape(R_NEW, 2 * DH)
    whole = got[:, 0:TOK, :].reshape(BLOCK, 2 * DH)
    last = s == SEQ - 1
    sink = jnp.where(
        s == 0,
        cache[0:SINKS],
        jnp.where(s == 4, second[0:SINKS], jnp.where(s == 8, first[0:SINKS], third[0:SINKS])),
    )
    for out in (own, two_on, odd_on):
        out[BLOCK:, :] = sink
    own[0:BLOCK, :] = whole
    for shift, over in ((two_on, s + 2 >= SEQ), (odd_on, (s % 2 == 1) & (s + 3 >= SEQ))):

        @pl.when(jnp.logical_not(over))
        def _():
            shift[0:BLOCK, :] = whole

        @pl.when(over)
        def _():
            shift[0:PRE, :] = first[...]
            shift[PRE:BLOCK, :] = jnp.where(last, cache[...], second[...])


def pack_q_kernel(flags, place, q, out, *rings):
    low, high = retrieval_groups(flags)
    for k, ring in enumerate(rings):
        other = (place[1] + k) % RING
        start = pl.multiple_of(jnp.where(other // KEY_PARTS == 0, low, high) * WIDE, WIDE)
        ring[...] = q[:, pl.ds(start, WIDE)]
    for h in range(HEAD):
        out[h] = q[:, h * WIDE : (h + 1) * WIDE]


P_TILE = 256
P_SPAN = WINDOW_BLOCKS * BLOCK + P_TILE
P_KEYS = P_SPAN + DH


def passing_kernel(place, flags, sinks, windows, q, far, two, near, own, out, kbuf, vbuf, kt, vt, bias):
    s, h = place[0], place[1]
    odd = s % 2

    @pl.when(flags[h] == 0)
    def _():
        n_sink, window = sinks[h], windows[h]
        for i, b in ((2 * odd, near), (1, two), (2 - 2 * odd, far), (3, own)):
            rows = pl.ds(pl.multiple_of(i * BLOCK, BLOCK), BLOCK)
            kbuf[rows, :] = b[0:BLOCK, 0:DH]
            vbuf[rows, :] = b[0:BLOCK, DH:]
        sink = own[BLOCK:, :]
        for i, b in ((1, near), (2, two), (3, far)):
            sink = jnp.where(s % 4 == i, b[BLOCK:, :], sink)
        kt[P_SPAN : P_SPAN + SINKS, :] = sink[:, 0:DH]
        kt[P_SPAN + SINKS :, :] = jnp.zeros((DH - SINKS, DH), bf16)
        vt[P_SPAN : P_SPAN + SINKS, 0:DH] = sink[:, DH:]
        vt[P_SPAN + SINKS :, 0:DH] = jnp.zeros((DH - SINKS, DH), bf16)
        vt[:, DH:] = jnp.ones((P_KEYS, DH), bf16)

        def tile(t, _):
            rows = pl.ds(pl.multiple_of(t * P_TILE, P_TILE), P_SPAN)
            kt[0:P_SPAN, :] = kbuf[rows, :]
            vt[0:P_SPAN, 0:DH] = vbuf[rows, :]
            row = lax.broadcasted_iota(jnp.int32, (P_TILE, P_KEYS), 0) + WINDOW_BLOCKS * BLOCK
            col = lax.broadcasted_iota(jnp.int32, (P_TILE, P_KEYS), 1)
            seen = jnp.where(
                col < P_SPAN,
                jnp.where((col <= row) & (col > row - window), 0.0, HIDDEN),
                jnp.where(col - P_SPAN < n_sink, 0.0, HIDDEN),
            )
            bias[...] = seen
            places = pl.ds(t * (P_TILE // TOK), P_TILE // TOK)

            def scores(i):
                qi = q[places, :, i * DH : (i + 1) * DH].reshape(P_TILE, DH)
                return lax.dot_general(qi, kt[...], NT, preferred_element_type=f32)

            s = scores(0)
            for i in range(GROUP):
                ahead = scores(i + 1) if i + 1 < GROUP else None
                s = s + bias[...]
                top = jnp.max(s, -1, keepdims=True)
                p = jnp.exp2(s * LOG2E_SCALED - top * LOG2E_SCALED).astype(bf16)
                acc = jnp.dot(p, vt[...], preferred_element_type=f32)
                o = (acc[:, 0:DH] / acc[:, DH:]).astype(bf16)
                out[places, :, i * DH : (i + 1) * DH] = o.reshape(P_TILE // TOK, TOK, DH)
                s = ahead
            return 0

        lax.fori_loop(0, BLOCK // P_TILE, tile, 0)


R_CHUNK = 1024
R_KEYS = SEQ * R_ROWS // 2
R_QUERIES = 2 * PIECE


def retrieval_kernel(own_core, place, *refs):
    rings, refs = refs[:RING], refs[RING:]
    if own_core:
        *chunks, acc, top, kbuf, vbuf, qbuf, bias = refs
    else:
        *chunks, old_acc, old_top, out, kbuf, vbuf, qbuf, acc, top = refs
    s, h = place[0], place[1]
    part = h % KEY_PARTS
    y, zc = s // 4, s % 4
    core = zc % 2 if own_core else 1 - zc % 2
    diagonal = R_NEW if own_core else 0
    fixed = diagonal + SEQ // 2 * R_PRE
    vbuf[:, DH:] = jnp.ones((R_KEYS, DH), bf16)
    for back, chunk in enumerate(chunks):
        for dz in range(2):
            zh = zc // 2 if dz == 0 else 1 - zc // 2
            pair = ((y + 4 - back) % 4) * 2 + zh
            other = 2 * pair + core
            base = dz * R_ROWS
            to = diagonal + (2 * back + dz) * R_PRE
            kbuf[to : to + R_PRE, :] = chunk[base : base + R_PRE, 0:DH]
            vbuf[to : to + R_PRE, 0:DH] = chunk[base : base + R_PRE, DH:]
            new = chunk[base + R_PRE : base + R_ROWS, :]
            if own_core and back == 0 and dz == 0:
                kbuf[0:R_NEW, :] = new[:, 0:DH]
                vbuf[0:R_NEW, 0:DH] = new[:, DH:]
            new = jnp.where(other < s, new, jnp.zeros_like(new))

            @pl.when(fixed + pair * R_NEW < R_KEYS)
            def _():
                to = pl.ds(pl.multiple_of(fixed + pair * R_NEW, R_NEW), R_NEW)
                kbuf[to, :] = new[:, 0:DH]
                vbuf[to, 0:DH] = new[:, DH:]

    for k, ring in enumerate(rings):
        x = (h + RING - k) % RING
        for i in range(GROUP):
            to = pl.ds(pl.multiple_of((i % 2) * PIECE + x * TOK, TOK), TOK)
            qbuf[i // 2, to, :] = ring[:, i * DH : (i + 1) * DH]
    count = fixed + (s // 2 + (0 if own_core else zc % 2)) * R_NEW
    steps = (count + R_CHUNK - 1) // R_CHUNK
    if own_core:
        token = lax.broadcasted_iota(jnp.int32, (R_QUERIES, R_NEW), 0) % PIECE + (h // RING) * PIECE
        col = lax.broadcasted_iota(jnp.int32, (R_QUERIES, R_NEW), 1)
        key = (col // R_NEW_DEV) * TOK + part * R_NEW_DEV + col % R_NEW_DEV
        bias[...] = jnp.where(key <= token, 0.0, HIDDEN)
    else:
        acc[...] = old_acc[...]
        top[...] = old_top[...]

    def scores(i, keys):
        return lax.dot_general(qbuf[i], keys, NT, preferred_element_type=f32)

    def step(j, kind):
        if kind == "first":
            rows = slice(0, R_CHUNK)
        else:
            rows = pl.ds(pl.multiple_of(j * R_CHUNK, R_CHUNK), R_CHUNK)
        keys = kbuf[rows, :]
        values = vbuf[rows, :]
        if kind == "last":
            at = lax.broadcasted_iota(jnp.int32, (1, R_CHUNK), 1) + j * R_CHUNK
            tail = jnp.where(at < count, 0.0, HIDDEN)
        s_now = scores(0, keys)
        for i in range(R_UNITS):
            ahead = scores(i + 1, keys) if i + 1 < R_UNITS else None
            if kind == "first":
                s_now = jnp.concatenate([s_now[:, 0:R_NEW] + bias[...], s_now[:, R_NEW:]], 1)
            if kind == "last":
                s_now = s_now + tail
            peak = jnp.max(s_now, -1, keepdims=True)
            if kind == "first":
                fresh = peak
            else:
                old = top[i][:, 0:1]
                fresh = jnp.maximum(old, peak)
                shrink = jnp.exp2((old - fresh) * LOG2E_SCALED)
            p = jnp.exp2(s_now * LOG2E_SCALED - fresh * LOG2E_SCALED).astype(bf16)
            d = jnp.dot(p, values, preferred_element_type=f32)
            if kind != "first":
                d = acc[i] * shrink + d
            top[i] = jnp.broadcast_to(fresh, (R_QUERIES, DH))
            acc[i] = d
            s_now = ahead

    def middle(j, _):
        step(j, "middle")
        return 0

    if own_core:
        step(0, "first")
    lax.fori_loop(1 if own_core else 0, steps - 1, middle, 0)
    step(steps - 1, "last")
    if own_core:
        return

    lane = lax.broadcasted_iota(jnp.int32, (PIECE, DH), 1)
    logs = jnp.zeros((PIECE, DH), f32)
    for i in range(GROUP):
        rows = slice((i % 2) * PIECE, (i % 2 + 1) * PIECE)
        total = acc[i // 2, rows, DH:]
        o = (acc[i // 2, rows, 0:DH] / total).astype(bf16)
        out[:, :, i * DH : (i + 1) * DH] = o.reshape(RING, TOK, DH)
        log = top[i // 2, rows] * LOG2E_SCALED + jnp.log2(total)
        hi = log.astype(bf16).astype(f32)
        mid = (log - hi).astype(bf16).astype(f32)
        lo = log - hi - mid
        logs = jnp.where(lane == 3 * i, hi, logs)
        logs = jnp.where(lane == 3 * i + 1, mid, logs)
        logs = jnp.where(lane == 3 * i + 2, lo, logs)
    out[:, :, WIDE:] = logs.astype(bf16).reshape(RING, TOK, DH)


def finish_kernel(flags, passing, partial, out):
    groups = retrieval_groups(flags)
    for g in range(KVH):

        @pl.when(flags[g] == 0)
        def _():
            out[:, g * WIDE : (g + 1) * WIDE] = passing[g]

    for which in range(2):
        pieces = [partial[which * KEY_PARTS + kp] for kp in range(KEY_PARTS)]
        for i in range(GROUP):
            logs = []
            for piece in pieces:
                l3 = piece[:, WIDE + 3 * i : WIDE + 3 * i + 3].astype(f32)
                logs.append(l3[:, 0:1] + l3[:, 1:2] + l3[:, 2:3])
            top = functools.reduce(jnp.maximum, logs)
            shares = [jnp.exp2(x - top) for x in logs]
            total = functools.reduce(jnp.add, shares)
            o = sum(
                piece[:, i * DH : (i + 1) * DH].astype(f32) * (share / total)
                for piece, share in zip(pieces, shares)
            )
            start = groups[which] * WIDE + i * DH
            out[:, pl.ds(pl.multiple_of(start, DH), DH)] = o.astype(bf16)


def swap(x, axis):
    return lax.all_to_all(x, axis, split_axis=0, concat_axis=0, tiled=True)


def body(queries, new_keys, new_values, cache_keys, cache_values, retrieval, sinks, windows):
    column_index = lax.axis_index("zl") * RING + lax.axis_index("x")
    place = jnp.stack([lax.axis_index("seq"), column_index]).astype(jnp.int32)

    def send(x, pairs):
        return lax.ppermute(x, "seq", pairs)

    sds = jax.ShapeDtypeStruct
    two = 2 * DH
    packed, cache = call(
        pack_kv_kernel,
        (sds((HEAD, TOK + R_SEND, two), bf16), sds((PRE, two), bf16)),
        (retrieval, new_keys, new_values, cache_keys, cache_values),
        vmem=60,
    )
    got = swap(packed, ("zl", "x"))
    first = send(cache, [(10, 13), (12, 14), (14, 15), (0, 8)])
    second = send(cache, [(11, 13), (13, 14), (0, 4)])
    third = send(cache, [(0, 12)])
    ring = sds((TOK, WIDE), bf16)
    packed_q, *rings = call(
        pack_q_kernel,
        (sds((HEAD, TOK, WIDE), bf16), ring, ring, ring, ring),
        (retrieval, place, queries),
        nbytes=2**22,
        vmem=60,
    )
    rings = rings[:1] + [
        lax.ppermute(rings[k], "x", [(i, (i + k) % RING) for i in range(RING)]) for k in (1, 2, 3)
    ]
    got, first, second, third, packed_q, *rings = lax.optimization_barrier(
        (got, first, second, third, packed_q, *rings)
    )
    rows = sds((CARRY, two), bf16)
    part, own, two_on, odd_on = call(
        unpack_kv_kernel,
        (sds((R_ROWS, two), bf16), rows, rows, rows),
        (retrieval, place, got, cache, first, second, third),
    )
    cells = [(y, zh, c) for y in range(4) for zh in range(2) for c in range(2)]
    back_z = send(part, [(4 * y + 2 * z + c, 4 * y + 2 * (1 - z) + c) for y, z, c in cells])
    column = jnp.concatenate([part, back_z], 0)
    own_core = [column] + [send(column, [(i, (i + 4 * k) % SEQ) for i in range(SEQ)]) for k in (1, 2, 3)]
    two_on, odd_on, packed_q, own_core[1] = lax.optimization_barrier(
        (two_on, odd_on, packed_q, own_core[1])
    )
    q = swap(packed_q, ("zl", "x"))
    back_two = send(two_on, [(i, (i + 2) % SEQ) for i in range(SEQ)])
    near = send(odd_on, [(i, i + 1 if i % 2 == 0 else (i + 3) % SEQ) for i in range(SEQ)])
    other_core = [send(x, [(i, i ^ 1) for i in range(SEQ)]) for x in own_core]

    state = [
        sds((R_UNITS, R_QUERIES, 2 * DH), f32),
        sds((R_UNITS, R_QUERIES, DH), f32),
    ]
    buffers = [
        pltpu.VMEM((R_KEYS, DH), bf16),
        pltpu.VMEM((R_KEYS, 2 * DH), bf16),
        pltpu.VMEM((R_UNITS, R_QUERIES, DH), bf16),
    ]
    flops = R_UNITS * R_QUERIES * R_KEYS * 4 * DH
    acc, top = call(
        functools.partial(retrieval_kernel, True),
        state,
        (place, *rings, *own_core),
        flops=flops,
        nbytes=2**22,
        scratch=buffers + [pltpu.VMEM((R_QUERIES, R_NEW), f32)],
    )
    acc, top, back_two, *other_core = lax.optimization_barrier((acc, top, back_two, *other_core))
    far = send(back_two, [(i, i ^ 1) for i in range(SEQ)])
    partial = call(
        functools.partial(retrieval_kernel, False),
        sds((RING, TOK, R_LANES), bf16),
        (place, *rings, *other_core, acc, top),
        flops=flops,
        nbytes=2**22,
        scratch=buffers + [pltpu.VMEM(a.shape, f32) for a in state],
    )
    partial, q, far, near = lax.optimization_barrier((partial, q, far, near))
    partial_back = swap(partial, "x")
    pairs = BLOCK * GROUP * P_KEYS
    passing = call(
        passing_kernel,
        sds((HEAD, TOK, WIDE), bf16),
        (place, retrieval, sinks, windows, q, far, back_two, near, own),
        flops=pairs * 4 * DH,
        nbytes=2**22,
        scratch=[
            pltpu.VMEM((4 * BLOCK, DH), bf16),
            pltpu.VMEM((4 * BLOCK, DH), bf16),
            pltpu.VMEM((P_KEYS, DH), bf16),
            pltpu.VMEM((P_KEYS, 2 * DH), bf16),
            pltpu.VMEM((P_TILE, P_KEYS), f32),
        ],
    )
    passing, partial_back = lax.optimization_barrier((passing, partial_back))
    passing_back = swap(passing, ("zl", "x"))
    step = TOK // 4
    return pl.pallas_call(
        finish_kernel,
        grid=(TOK // step,),
        out_shape=sds((TOK, HQ * DH), bf16),
        in_specs=[
            SMEM,
            pl.BlockSpec((HEAD, step, WIDE), lambda i: (0, i, 0)),
            pl.BlockSpec((RING, step, R_LANES), lambda i: (0, i, 0)),
        ],
        out_specs=pl.BlockSpec((step, HQ * DH), lambda i: (i, 0)),
        compiler_params=pltpu.CompilerParams(vmem_limit_bytes=56 * 2**20),
        cost_estimate=pl.CostEstimate(flops=0, bytes_accessed=2**22, transcendentals=0),
    )(retrieval, passing_back, partial_back)


def solution(mesh):
    cut = jax.sharding.Mesh(mesh.devices.reshape(SEQ, 2, RING), ("seq", "zl", "x"))
    tokens = P(("seq", "zl", "x"), None)
    cache = P("seq", ("zl", "x"))
    return jax.shard_map(
        body,
        mesh=cut,
        in_specs=(tokens, tokens, tokens, cache, cache, P(), P(), P()),
        out_specs=tokens,
        check_vma=False,
    )
```

```python
import functools
import math

import jax
import jax.numpy as jnp
from jax import lax
from jax.experimental import pallas as pl
from jax.experimental.pallas import tpu as pltpu
from jax.sharding import PartitionSpec as P

HQ = 64
KVH = 8
DH = 128
GROUP = HQ // KVH
WIDE = GROUP * DH
SINKS = 64

SEQ, HEAD = 16, 8
TOK = 64
BLOCK = TOK * HEAD
PRE = 256
CARRY = BLOCK + SINKS
WINDOW_BLOCKS = 3

RING = 4
KEY_PARTS = 2
PIECE = TOK * RING
R_NEW_DEV = TOK // KEY_PARTS
R_NEW = BLOCK // KEY_PARTS
R_PRE = PRE // KEY_PARTS
R_SEND = R_NEW_DEV + R_PRE
R_ROWS = R_NEW + R_PRE
R_UNITS = 4
R_LANES = WIDE + DH

LOG2E_SCALED = math.log2(math.e) / math.sqrt(DH)
HIDDEN = -1e30
NT = (((1,), (1,)), ((), ()))

SMEM = pl.BlockSpec(memory_space=pltpu.SMEM)
bf16 = jnp.bfloat16
f32 = jnp.float32


VMEM = pl.BlockSpec(memory_space=pltpu.VMEM)
ANY = pl.BlockSpec(memory_space=pl.ANY)


def call(kernel, outs, ins, flops=0, nbytes=2**20, scratch=(), vmem=24, by_hand=False, resident=()):
    def spec(a, kept):
        if a.dtype == jnp.int32:
            return SMEM
        if kept:
            return VMEM
        return ANY if by_hand else pl.BlockSpec(a.shape, lambda i: (0,) * len(a.shape))

    listed = outs if isinstance(outs, (tuple, list)) else (outs,)
    kept_in = [any(a is r for r in resident) for a in ins]
    kept_out = [any(a is r for r in resident) for a in listed]
    return pl.pallas_call(
        kernel,
        grid=(1,),
        out_shape=outs,
        in_specs=[spec(a, k) for a, k in zip(ins, kept_in)],
        out_specs=jax.tree.unflatten(jax.tree.structure(outs), [spec(a, k) for a, k in zip(listed, kept_out)]),
        scratch_shapes=list(scratch),
        compiler_params=pltpu.CompilerParams(vmem_limit_bytes=vmem * 2**20),
        cost_estimate=pl.CostEstimate(flops=flops, bytes_accessed=nbytes, transcendentals=0),
    )(*ins)


def retrieval_groups(flags):
    low = jnp.int32(0)
    high = jnp.int32(0)
    for g in range(KVH):
        high = jnp.where(flags[g] == 1, g, high)
        low = jnp.where(flags[KVH - 1 - g] == 1, KVH - 1 - g, low)
    return low, high


def pack_kv_kernel(flags, nk, nv, ck, cv, out, cache):
    groups = retrieval_groups(flags)
    cache[:, 0:DH] = ck[...]
    cache[:, DH:] = cv[...]
    for h in range(HEAD):
        out[h, 0:TOK, 0:DH] = nk[:, h * DH : (h + 1) * DH]
        out[h, 0:TOK, DH:] = nv[:, h * DH : (h + 1) * DH]
        x = h % RING
        cols = pl.ds(pl.multiple_of(groups[x // KEY_PARTS] * DH, DH), DH)
        part = x % KEY_PARTS
        rows = slice(part * R_NEW_DEV, (part + 1) * R_NEW_DEV)
        end = TOK + R_NEW_DEV
        out[h, TOK:end, 0:DH] = nk[rows, cols]
        out[h, TOK:end, DH:] = nv[rows, cols]
        rows = slice(part * R_PRE, (part + 1) * R_PRE)
        out[h, end:, 0:DH] = ck[rows, :]
        out[h, end:, DH:] = cv[rows, :]


def unpack_kv_kernel(flags, place, got, cache, first, second, third, part, own, two_on, odd_on, even_on):
    s = place[0]
    low, high = retrieval_groups(flags)
    source = jnp.where((place[1] % RING) // KEY_PARTS == 0, low, high)
    end = TOK + R_NEW_DEV
    part[0:R_PRE, :] = got[source, end:, :]
    part[R_PRE:, :] = got[:, TOK:end, :].reshape(R_NEW, 2 * DH)
    whole = got[:, 0:TOK, :].reshape(BLOCK, 2 * DH)
    last = s == SEQ - 1
    sink = jnp.where(
        s == 0,
        cache[0:SINKS],
        jnp.where(s == 4, second[0:SINKS], jnp.where(s == 8, first[0:SINKS], third[0:SINKS])),
    )
    own[0:BLOCK, :] = whole
    own[BLOCK:, :] = sink
    odd = s % 2
    for shift, by in ((two_on, 2), (odd_on, 1 + 2 * odd), (even_on, 3 - 2 * odd)):
        shift[BLOCK:, :] = sink

        @pl.when(s + by < SEQ)
        def _():
            shift[0:BLOCK, :] = whole

        @pl.when(s + by >= SEQ)
        def _():
            shift[0:PRE, :] = first[...]
            shift[PRE:BLOCK, :] = jnp.where(last, cache[...], second[...])


def pack_q_kernel(flags, place, q, out, *rings):
    low, high = retrieval_groups(flags)
    for k, ring in enumerate(rings):
        other = (place[1] + k) % RING
        start = pl.multiple_of(jnp.where(other // KEY_PARTS == 0, low, high) * WIDE, WIDE)
        ring[...] = q[:, pl.ds(start, WIDE)]
    for h in range(HEAD):
        out[h] = q[:, h * WIDE : (h + 1) * WIDE]


P_TILE = 256
P_SPAN = WINDOW_BLOCKS * BLOCK + P_TILE
P_KEYS = P_SPAN + DH


def passing_kernel(place, flags, sinks, windows, q, far, two, near, own, out, kbuf, vbuf, kt, vt, qbuf, obuf, bias, kv_sems, q_sems, out_sems):
    s, h = place[0], place[1]
    odd = s % 2
    tiles = BLOCK // P_TILE

    @pl.when(flags[h] == 0)
    def _():
        n_sink, window = sinks[h], windows[h]

        def load(block, rows, sem):
            return [
                pltpu.make_async_copy(block.at[0:BLOCK, 0:DH], kbuf.at[rows], kv_sems.at[sem]),
                pltpu.make_async_copy(block.at[0:BLOCK, DH : 2 * DH], vbuf.at[rows], kv_sems.at[sem + 1]),
            ]

        copies = []
        for i, (at, block) in enumerate(((2 * odd, near), (1, two), (2 - 2 * odd, far), (3, own))):
            copies += load(block, pl.ds(pl.multiple_of(at * BLOCK, BLOCK), BLOCK), 2 * i)
        for copy in copies:
            copy.start()

        def load_sinks(block):
            rows = pl.ds(P_SPAN, SINKS)
            return [
                pltpu.make_async_copy(block.at[BLOCK:CARRY, 0:DH], kt.at[rows], kv_sems.at[8]),
                pltpu.make_async_copy(block.at[BLOCK:CARRY, DH : 2 * DH], vt.at[rows, 0:DH], kv_sems.at[9]),
            ]

        for i, block in enumerate((own, near, two, far)):

            @pl.when(s % 4 == i)
            def _():
                for copy in load_sinks(block):
                    copy.start()

        queries = []
        for i in range(GROUP):
            cols = slice(i * DH, (i + 1) * DH)
            queries.append(pltpu.make_async_copy(q.at[:, :, cols], qbuf.at[:, :, cols], q_sems.at[i]))
            queries[-1].start()
        kt[P_SPAN + SINKS :, :] = jnp.zeros((DH - SINKS, DH), bf16)
        vt[P_SPAN + SINKS :, 0:DH] = jnp.zeros((DH - SINKS, DH), bf16)
        vt[:, DH:] = jnp.ones((P_KEYS, DH), bf16)

        def give(t, i):
            places, cols = pl.ds(t * (P_TILE // TOK), P_TILE // TOK), slice(i * DH, (i + 1) * DH)
            return pltpu.make_async_copy(obuf.at[places, :, cols], out.at[places, :, cols], out_sems.at[t, i])

        def tile(t, _):
            row = lax.broadcasted_iota(jnp.int32, (P_TILE, P_KEYS), 0) + WINDOW_BLOCKS * BLOCK
            col = lax.broadcasted_iota(jnp.int32, (P_TILE, P_KEYS), 1)
            bias[...] = jnp.where(
                col < P_SPAN,
                jnp.where((col <= row) & (col > row - window), 0.0, HIDDEN),
                jnp.where(col - P_SPAN < n_sink, 0.0, HIDDEN),
            )

            @pl.when(t == 0)
            def _():
                for copy in copies + load_sinks(own) + queries:
                    copy.wait()

            rows = pl.ds(pl.multiple_of(t * P_TILE, P_TILE), P_SPAN)
            kt[0:P_SPAN, :] = kbuf[rows, :]
            vt[0:P_SPAN, 0:DH] = vbuf[rows, :]
            places = pl.ds(t * (P_TILE // TOK), P_TILE // TOK)

            def scores(i):
                qi = qbuf[places, :, i * DH : (i + 1) * DH].reshape(P_TILE, DH)
                return lax.dot_general(qi, kt[...], NT, preferred_element_type=f32)

            s_now = scores(0)
            for i in range(GROUP):
                ahead = scores(i + 1) if i + 1 < GROUP else None
                s_now = s_now + bias[...]
                top = jnp.max(s_now, -1, keepdims=True)
                p = jnp.exp2(s_now * LOG2E_SCALED - top * LOG2E_SCALED).astype(bf16)
                acc = jnp.dot(p, vt[...], preferred_element_type=f32)
                o = (acc[:, 0:DH] / acc[:, DH:]).astype(bf16)
                obuf[places, :, i * DH : (i + 1) * DH] = o.reshape(P_TILE // TOK, TOK, DH)
                give(t, i).start()
                s_now = ahead
            return 0

        lax.fori_loop(0, tiles, tile, 0)
        for t in range(tiles):
            for i in range(GROUP):
                give(t, i).wait()


R_CHUNK = 768
R_KEYS = 3 * R_CHUNK
R_QUERIES = 2 * PIECE


def retrieval_kernel(phase, place, *refs):
    if phase == 0:
        (*rings, column, across), (acc, top, qbuf), (kbuf, vbuf, sems, bias, ring_sems) = refs[:6], refs[6:9], refs[9:]
        chunks = column, across
    elif phase == 1:
        (*chunks, qbuf, old_acc, old_top), (acc, top), (kbuf, vbuf, sems) = refs[:6], refs[6:8], refs[8:]
    else:
        (*chunks, qbuf, old_acc, old_top), (out,), (kbuf, vbuf, sems, acc, top, obuf, out_sems) = refs[:6], refs[6:7], refs[7:]
    s, h = place[0], place[1]
    part = h % KEY_PARTS
    y, zh, core = s // 4, (s // 2) % 2, s % 2
    diagonal = R_NEW if phase == 0 else 0
    kbuf[R_CHUNK:, :] = jnp.zeros((R_KEYS - R_CHUNK, DH), bf16)
    vbuf[R_CHUNK:, 0:DH] = jnp.zeros((R_KEYS - R_CHUNK, DH), bf16)
    vbuf[:, DH:] = jnp.ones((R_KEYS, DH), bf16)

    def fetch(chunk, base, to, rows, sem):
        return [
            pltpu.make_async_copy(chunk.at[base : base + rows, 0:DH], kbuf.at[pl.ds(to, rows)], sems.at[sem]),
            pltpu.make_async_copy(
                chunk.at[base : base + rows, DH : 2 * DH], vbuf.at[pl.ds(to, rows), 0:DH], sems.at[sem + 1]
            ),
        ]

    at_once, later = [], []
    for i, chunk in enumerate(chunks):
        for dz in range(2):
            their_zh = zh if dz == 0 else 1 - zh
            if phase == 0:
                slot = 2 * their_zh + (core if i == 0 else 1 - core)
                seen = slot < s % 4
            else:
                their_y = (y + 3 - i) % 4
                slot = 2 * their_y + their_zh
                seen = their_y < y
            base = dz * R_ROWS
            sem = 4 * (2 * i + dz)
            at_once += fetch(chunk, base, diagonal + (2 * i + dz) * R_PRE, R_PRE, sem)
            if phase == 0 and i == 0 and dz == 0:
                at_once += fetch(chunk, base + R_PRE, 0, R_NEW, sem + 2)
            else:
                to = pl.multiple_of(R_CHUNK + slot * R_NEW, R_NEW)
                later.append((seen, fetch(chunk, base + R_PRE, to, R_NEW, sem + 2)))
    if phase == 0:
        for k, ring in enumerate(rings):
            x = (h + RING - k) % RING
            for i in range(GROUP):
                to = pl.ds(pl.multiple_of((i % 2) * PIECE + x * TOK, TOK), TOK)
                at_once.append(
                    pltpu.make_async_copy(
                        ring.at[:, i * DH : (i + 1) * DH], qbuf.at[i // 2, to], ring_sems.at[k * GROUP + i]
                    )
                )
    for copy in at_once:
        copy.start()
    for seen, copies in later:

        @pl.when(seen)
        def _():
            for copy in copies:
                copy.start()

    count = R_CHUNK + (s % 4 if phase == 0 else 2 * y) * R_NEW
    if phase == 0:
        token = lax.broadcasted_iota(jnp.int32, (R_QUERIES, R_NEW), 0) % PIECE + (h // RING) * PIECE
        col = lax.broadcasted_iota(jnp.int32, (R_QUERIES, R_NEW), 1)
        key = (col // R_NEW_DEV) * TOK + part * R_NEW_DEV + col % R_NEW_DEV
        bias[...] = jnp.where(key <= token, 0.0, HIDDEN)

    def scores(i, keys):
        return lax.dot_general(qbuf[i], keys, NT, preferred_element_type=f32)

    def step(j, kind):
        if kind in ("diagonal", "first"):
            rows = slice(0, R_CHUNK)
        else:
            rows = pl.ds(pl.multiple_of(j * R_CHUNK, R_CHUNK), R_CHUNK)
        keys = kbuf[rows, :]
        values = vbuf[rows, :]
        before, above = (old_acc, old_top) if kind == "first" else (acc, top)
        if kind == "last":
            at = lax.broadcasted_iota(jnp.int32, (1, R_CHUNK), 1) + j * R_CHUNK
            tail = jnp.where(at < count, 0.0, HIDDEN)
        s_now = scores(0, keys)
        for i in range(R_UNITS):
            ahead = scores(i + 1, keys) if i + 1 < R_UNITS else None
            if kind == "diagonal":
                s_now = jnp.concatenate([s_now[:, 0:R_NEW] + bias[...], s_now[:, R_NEW:]], 1)
            if kind == "last":
                s_now = s_now + tail
            fresh = jnp.broadcast_to(jnp.max(s_now, -1, keepdims=True), (R_QUERIES, DH))
            if kind != "diagonal":
                old = above[i]
                fresh = jnp.maximum(old, fresh)
                shrink = jnp.exp2((old - fresh) * LOG2E_SCALED)
            shift = jnp.concatenate([fresh * LOG2E_SCALED] * (R_CHUNK // DH), 1)
            p = jnp.exp2(s_now * LOG2E_SCALED - shift).astype(bf16)
            d = jnp.dot(p, values, preferred_element_type=f32)
            if kind != "diagonal":
                d = before[i] * jnp.concatenate([shrink, shrink], 1) + d
            top[i] = fresh
            acc[i] = d
            s_now = ahead

    def middle(j, _):
        step(j, "middle")
        return 0

    for copy in at_once:
        copy.wait()
    step(0, "diagonal" if phase == 0 else "first")
    for seen, copies in later:

        @pl.when(seen)
        def _():
            for copy in copies:
                copy.wait()

    lax.fori_loop(1, count // R_CHUNK, middle, 0)

    @pl.when(count % R_CHUNK > 0)
    def _():
        step(count // R_CHUNK, "last")

    if phase < 2:
        return

    lane = lax.broadcasted_iota(jnp.int32, (PIECE, DH), 1)
    logs = jnp.zeros((PIECE, DH), f32)
    copies = []

    def give(i):
        cols = slice(i * DH, (i + 1) * DH)
        copies.append(pltpu.make_async_copy(obuf.at[:, :, cols], out.at[:, :, cols], out_sems.at[i]))
        copies[-1].start()

    for i in range(GROUP):
        rows = slice((i % 2) * PIECE, (i % 2 + 1) * PIECE)
        total = acc[i // 2, rows, DH:]
        o = (acc[i // 2, rows, 0:DH] / total).astype(bf16)
        obuf[:, :, i * DH : (i + 1) * DH] = o.reshape(RING, TOK, DH)
        give(i)
        log = top[i // 2, rows] * LOG2E_SCALED + jnp.log2(total)
        hi = log.astype(bf16).astype(f32)
        mid = (log - hi).astype(bf16).astype(f32)
        lo = log - hi - mid
        logs = jnp.where(lane == 3 * i, hi, logs)
        logs = jnp.where(lane == 3 * i + 1, mid, logs)
        logs = jnp.where(lane == 3 * i + 2, lo, logs)
    obuf[:, :, WIDE:] = logs.astype(bf16).reshape(RING, TOK, DH)
    give(GROUP)
    for copy in copies:
        copy.wait()


def place_passing_kernel(flags, passing, _, out, sems):
    def copy(g):
        return pltpu.make_async_copy(passing.at[g], out.at[:, g * WIDE : (g + 1) * WIDE], sems.at[g])

    for g in range(KVH):

        @pl.when(flags[g] == 0)
        def _():
            copy(g).start()

    for g in range(KVH):

        @pl.when(flags[g] == 0)
        def _():
            copy(g).wait()


def merge_kernel(flags, partial, out, wide, sems):
    groups = retrieval_groups(flags)
    copies = []
    for which in range(2):
        pieces = [partial[which * KEY_PARTS + kp] for kp in range(KEY_PARTS)]
        logs3 = [piece[:, WIDE:].astype(f32) for piece in pieces]
        for i in range(GROUP):
            logs = [
                l[:, 3 * i : 3 * i + 1] + l[:, 3 * i + 1 : 3 * i + 2] + l[:, 3 * i + 2 : 3 * i + 3] for l in logs3
            ]
            top = functools.reduce(jnp.maximum, logs)
            shares = [jnp.exp2(x - top) for x in logs]
            total = functools.reduce(jnp.add, shares)
            o = sum(
                piece[:, i * DH : (i + 1) * DH].astype(f32) * (share / total)
                for piece, share in zip(pieces, shares)
            )
            wide[which, :, i * DH : (i + 1) * DH] = o.astype(bf16)
        columns = pl.ds(pl.multiple_of(groups[which] * WIDE, WIDE), WIDE)
        copies.append(pltpu.make_async_copy(wide.at[which], out.at[:, columns], sems.at[which]))
        copies[-1].start()
    for copy in copies:
        copy.wait()


def swap(x, axis):
    return lax.all_to_all(x, axis, split_axis=0, concat_axis=0, tiled=True)


def body(queries, new_keys, new_values, cache_keys, cache_values, retrieval, sinks, windows):
    column_index = lax.axis_index("zl") * RING + lax.axis_index("x")
    place = jnp.stack([lax.axis_index("seq"), column_index]).astype(jnp.int32)

    def send(x, pairs):
        return lax.ppermute(x, "seq", pairs)

    sds = jax.ShapeDtypeStruct
    two = 2 * DH
    packed, cache = call(
        pack_kv_kernel,
        (sds((HEAD, TOK + R_SEND, two), bf16), sds((PRE, two), bf16)),
        (retrieval, new_keys, new_values, cache_keys, cache_values),
        vmem=60,
    )
    got = swap(packed, ("zl", "x"))
    first = send(cache, [(10, 13), (12, 14), (14, 15), (0, 8)])
    second = send(cache, [(11, 13), (13, 14), (0, 4)])
    third = send(cache, [(0, 12)])
    ring = sds((TOK, WIDE), bf16)
    packed_q, *rings = call(
        pack_q_kernel,
        (sds((HEAD, TOK, WIDE), bf16), ring, ring, ring, ring),
        (retrieval, place, queries),
    )
    got, first, second, third, packed_q, *rings = lax.optimization_barrier(
        (got, first, second, third, packed_q, *rings)
    )
    rows = sds((CARRY, two), bf16)
    part, own, two_on, odd_on, even_on = call(
        unpack_kv_kernel,
        (sds((R_ROWS, two), bf16), rows, rows, rows, rows),
        (retrieval, place, got, cache, first, second, third),
    )
    cells = [(y, zh, c) for y in range(4) for zh in range(2) for c in range(2)]
    part, *rings = lax.optimization_barrier((part, *rings))
    back_z = send(part, [(4 * y + 2 * z + c, 4 * y + 2 * (1 - z) + c) for y, z, c in cells])
    rings = rings[:1] + [
        lax.ppermute(rings[k], "x", [(i, (i + k) % RING) for i in range(RING)]) for k in (1, 2, 3)
    ]
    column = jnp.concatenate([part, back_z], 0)
    column, packed_q = lax.optimization_barrier((column, packed_q))
    q = swap(packed_q, ("zl", "x"))
    own_core = [column] + [send(column, [(i, (i + 4 * k) % SEQ) for i in range(SEQ)]) for k in (1, 2, 3)]
    def other_core(x):
        return send(x, [(i, i ^ 1) for i in range(SEQ)])

    across = other_core(column)
    state = (
        sds((R_UNITS, R_QUERIES, 2 * DH), f32),
        sds((R_UNITS, R_QUERIES, DH), f32),
        sds((R_UNITS, R_QUERIES, DH), bf16),
    )
    dma = pltpu.SemaphoreType.DMA
    buffers = [
        pltpu.VMEM((R_KEYS, DH), bf16),
        pltpu.VMEM((R_KEYS, 2 * DH), bf16),
        dma((24,)),
    ]
    flops = R_UNITS * R_QUERIES * R_KEYS * 4 * DH
    acc, top, queried = call(
        functools.partial(retrieval_kernel, 0),
        state,
        (place, *rings, column, across),
        flops=flops,
        nbytes=2**22,
        scratch=buffers + [pltpu.VMEM((R_QUERIES, R_NEW), f32), dma((RING * GROUP,))],
        vmem=24,
        by_hand=True,
        resident=state,
    )
    same = own_core[1:]
    acc, two_on, odd_on, even_on, *same = lax.optimization_barrier((acc, two_on, odd_on, even_on, *same))
    other = [other_core(x) for x in same]
    back_two = send(two_on, [(i, (i + 2) % SEQ) for i in range(SEQ)])
    near = send(odd_on, [(i, (i + 1 + 2 * (i % 2)) % SEQ) for i in range(SEQ)])
    far = send(even_on, [(i, (i + 3 - 2 * (i % 2)) % SEQ) for i in range(SEQ)])
    acc, top = call(
        functools.partial(retrieval_kernel, 1),
        state[:2],
        (place, *same, queried, acc, top),
        flops=flops,
        nbytes=2**22,
        scratch=buffers,
        vmem=24,
        by_hand=True,
        resident=(*state, queried, acc, top),
    )
    acc, top, *other = lax.optimization_barrier((acc, top, *other))
    partial = call(
        functools.partial(retrieval_kernel, 2),
        sds((RING, TOK, R_LANES), bf16),
        (place, *other, queried, acc, top),
        flops=flops,
        nbytes=2**22,
        scratch=buffers
        + [pltpu.VMEM(a.shape, f32) for a in state[:2]]
        + [pltpu.VMEM((RING, TOK, R_LANES), bf16), dma((GROUP + 1,))],
        vmem=24,
        by_hand=True,
        resident=(queried, acc, top),
    )
    partial, q, far, near, back_two = lax.optimization_barrier((partial, q, far, near, back_two))
    partial_back = swap(partial, "x")
    passing = call(
        passing_kernel,
        sds((HEAD, TOK, WIDE), bf16),
        (place, retrieval, sinks, windows, q, far, back_two, near, own),
        flops=BLOCK * GROUP * P_KEYS * 4 * DH,
        nbytes=2**22,
        scratch=[
            pltpu.VMEM((4 * BLOCK, DH), bf16),
            pltpu.VMEM((4 * BLOCK, DH), bf16),
            pltpu.VMEM((P_KEYS, DH), bf16),
            pltpu.VMEM((P_KEYS, 2 * DH), bf16),
            pltpu.VMEM((HEAD, TOK, WIDE), bf16),
            pltpu.VMEM((HEAD, TOK, WIDE), bf16),
            pltpu.VMEM((P_TILE, P_KEYS), f32),
            dma((10,)),
            dma((GROUP,)),
            dma((BLOCK // P_TILE, GROUP)),
        ],
        vmem=58,
        by_hand=True,
    )
    passing, partial_back = lax.optimization_barrier((passing, partial_back))
    passing_back = swap(passing, ("zl", "x"))
    anywhere = pl.BlockSpec(memory_space=pl.ANY)
    result = sds((TOK, HQ * DH), bf16)
    merged = pl.pallas_call(
        merge_kernel,
        out_shape=result,
        in_specs=[SMEM, VMEM],
        out_specs=anywhere,
        scratch_shapes=[pltpu.VMEM((2, TOK, WIDE), bf16), pltpu.SemaphoreType.DMA((2,))],
        compiler_params=pltpu.CompilerParams(vmem_limit_bytes=44 * 2**20),
    )(retrieval, partial_back)
    return pl.pallas_call(
        place_passing_kernel,
        out_shape=result,
        in_specs=[SMEM, anywhere, anywhere],
        out_specs=anywhere,
        input_output_aliases={2: 0},
        scratch_shapes=[pltpu.SemaphoreType.DMA((KVH,))],
        compiler_params=pltpu.CompilerParams(vmem_limit_bytes=44 * 2**20),
    )(retrieval, passing_back, merged)


def solution(mesh):
    cut = jax.sharding.Mesh(mesh.devices.reshape(SEQ, 2, RING), ("seq", "zl", "x"))
    tokens = P(("seq", "zl", "x"), None)
    cache = P("seq", ("zl", "x"))
    return jax.shard_map(
        body,
        mesh=cut,
        in_specs=(tokens, tokens, tokens, cache, cache, P(), P(), P()),
        out_specs=tokens,
        check_vma=False,
    )
```

```python
import functools
import math

import jax
import jax.numpy as jnp
from jax import lax
from jax.experimental import pallas as pl
from jax.experimental.pallas import tpu as pltpu
from jax.sharding import PartitionSpec as P

HQ = 64
KVH = 8
DH = 128
GROUP = HQ // KVH
WIDE = GROUP * DH
SINKS = 64

SEQ, HEAD = 16, 8
TOK = 64
BLOCK = TOK * HEAD
PRE = 256
CARRY = BLOCK + SINKS
WINDOW_BLOCKS = 3

RING = 4
KEY_PARTS = 2
PIECE = TOK * RING
R_NEW_DEV = TOK // KEY_PARTS
R_NEW = BLOCK // KEY_PARTS
R_PRE = PRE // KEY_PARTS
R_SEND = R_NEW_DEV + R_PRE
R_ROWS = R_NEW + R_PRE
R_UNITS = 4
R_LANES = WIDE + DH

LOG2E_SCALED = math.log2(math.e) / math.sqrt(DH)
HIDDEN = -1e30
NT = (((1,), (1,)), ((), ()))

SMEM = pl.BlockSpec(memory_space=pltpu.SMEM)
bf16 = jnp.bfloat16
f32 = jnp.float32


VMEM = pl.BlockSpec(memory_space=pltpu.VMEM)
ANY = pl.BlockSpec(memory_space=pl.ANY)


def call(kernel, outs, ins, flops=0, nbytes=2**20, scratch=(), vmem=24, by_hand=False, resident=()):
    def spec(a, kept):
        if a.dtype == jnp.int32:
            return SMEM
        if kept:
            return VMEM
        return ANY if by_hand else pl.BlockSpec(a.shape, lambda i: (0,) * len(a.shape))

    listed = outs if isinstance(outs, (tuple, list)) else (outs,)
    kept_in = [any(a is r for r in resident) for a in ins]
    kept_out = [any(a is r for r in resident) for a in listed]
    return pl.pallas_call(
        kernel,
        grid=(1,),
        out_shape=outs,
        in_specs=[spec(a, k) for a, k in zip(ins, kept_in)],
        out_specs=jax.tree.unflatten(jax.tree.structure(outs), [spec(a, k) for a, k in zip(listed, kept_out)]),
        scratch_shapes=list(scratch),
        compiler_params=pltpu.CompilerParams(vmem_limit_bytes=vmem * 2**20),
        cost_estimate=pl.CostEstimate(flops=flops, bytes_accessed=nbytes, transcendentals=0),
    )(*ins)


def retrieval_groups(flags):
    low = jnp.int32(0)
    high = jnp.int32(0)
    for g in range(KVH):
        high = jnp.where(flags[g] == 1, g, high)
        low = jnp.where(flags[KVH - 1 - g] == 1, KVH - 1 - g, low)
    return low, high


def pack_kv_kernel(flags, nk, nv, ck, cv, out, cache):
    groups = retrieval_groups(flags)
    cache[:, 0:DH] = ck[...]
    cache[:, DH:] = cv[...]
    for h in range(HEAD):
        out[h, 0:TOK, 0:DH] = nk[:, h * DH : (h + 1) * DH]
        out[h, 0:TOK, DH:] = nv[:, h * DH : (h + 1) * DH]
        x = h % RING
        cols = pl.ds(pl.multiple_of(groups[x // KEY_PARTS] * DH, DH), DH)
        part = x % KEY_PARTS
        rows = slice(part * R_NEW_DEV, (part + 1) * R_NEW_DEV)
        end = TOK + R_NEW_DEV
        out[h, TOK:end, 0:DH] = nk[rows, cols]
        out[h, TOK:end, DH:] = nv[rows, cols]
        rows = slice(part * R_PRE, (part + 1) * R_PRE)
        out[h, end:, 0:DH] = ck[rows, :]
        out[h, end:, DH:] = cv[rows, :]


def unpack_kv_kernel(flags, place, got, cache, first, second, third, part, own, two_on, odd_on, even_on):
    s = place[0]
    low, high = retrieval_groups(flags)
    source = jnp.where((place[1] % RING) // KEY_PARTS == 0, low, high)
    end = TOK + R_NEW_DEV
    part[0:R_PRE, :] = got[source, end:, :]
    part[R_PRE:, :] = got[:, TOK:end, :].reshape(R_NEW, 2 * DH)
    whole = got[:, 0:TOK, :].reshape(BLOCK, 2 * DH)
    last = s == SEQ - 1
    sink = jnp.where(
        s == 0,
        cache[0:SINKS],
        jnp.where(s == 4, second[0:SINKS], jnp.where(s == 8, first[0:SINKS], third[0:SINKS])),
    )
    own[0:BLOCK, :] = whole
    own[BLOCK:, :] = sink
    odd = s % 2
    for shift, by in ((two_on, 2), (odd_on, 1 + 2 * odd), (even_on, 3 - 2 * odd)):
        shift[BLOCK:, :] = sink

        @pl.when(s + by < SEQ)
        def _():
            shift[0:BLOCK, :] = whole

        @pl.when(s + by >= SEQ)
        def _():
            shift[0:PRE, :] = first[...]
            shift[PRE:BLOCK, :] = jnp.where(last, cache[...], second[...])


def pack_q_kernel(flags, place, q, out, *rings):
    low, high = retrieval_groups(flags)
    for k, ring in enumerate(rings):
        other = (place[1] + k) % RING
        start = pl.multiple_of(jnp.where(other // KEY_PARTS == 0, low, high) * WIDE, WIDE)
        ring[...] = q[:, pl.ds(start, WIDE)]
    for h in range(HEAD):
        out[h] = q[:, h * WIDE : (h + 1) * WIDE]


P_TILE = 256
P_SPAN = WINDOW_BLOCKS * BLOCK + P_TILE
P_KEYS = P_SPAN + DH


def passing_kernel(place, flags, sinks, windows, q, far, two, near, own, out, kbuf, vbuf, kt, vt, qbuf, obuf, bias, kv_sems, q_sems, out_sems):
    s, h = place[0], place[1]
    odd = s % 2
    tiles = BLOCK // P_TILE

    @pl.when(flags[h] == 0)
    def _():
        n_sink, window = sinks[h], windows[h]

        def load(block, rows, sem):
            return [
                pltpu.make_async_copy(block.at[0:BLOCK, 0:DH], kbuf.at[rows], kv_sems.at[sem]),
                pltpu.make_async_copy(block.at[0:BLOCK, DH : 2 * DH], vbuf.at[rows], kv_sems.at[sem + 1]),
            ]

        copies = []
        for i, (at, block) in enumerate(((2 * odd, near), (1, two), (2 - 2 * odd, far), (3, own))):
            copies += load(block, pl.ds(pl.multiple_of(at * BLOCK, BLOCK), BLOCK), 2 * i)
        for copy in copies:
            copy.start()

        def load_sinks(block):
            rows = pl.ds(P_SPAN, SINKS)
            return [
                pltpu.make_async_copy(block.at[BLOCK:CARRY, 0:DH], kt.at[rows], kv_sems.at[8]),
                pltpu.make_async_copy(block.at[BLOCK:CARRY, DH : 2 * DH], vt.at[rows, 0:DH], kv_sems.at[9]),
            ]

        for i, block in enumerate((own, near, two, far)):

            @pl.when(s % 4 == i)
            def _():
                for copy in load_sinks(block):
                    copy.start()

        queries = []
        for i in range(GROUP):
            cols = slice(i * DH, (i + 1) * DH)
            queries.append(pltpu.make_async_copy(q.at[:, :, cols], qbuf.at[:, :, cols], q_sems.at[i]))
            queries[-1].start()
        kt[P_SPAN + SINKS :, :] = jnp.zeros((DH - SINKS, DH), bf16)
        vt[P_SPAN + SINKS :, 0:DH] = jnp.zeros((DH - SINKS, DH), bf16)
        vt[:, DH:] = jnp.ones((P_KEYS, DH), bf16)

        def give(t, i):
            places, cols = pl.ds(t * (P_TILE // TOK), P_TILE // TOK), slice(i * DH, (i + 1) * DH)
            return pltpu.make_async_copy(obuf.at[places, :, cols], out.at[places, :, cols], out_sems.at[t, i])

        def tile(t, _):
            row = lax.broadcasted_iota(jnp.int32, (P_TILE, P_KEYS), 0) + WINDOW_BLOCKS * BLOCK
            col = lax.broadcasted_iota(jnp.int32, (P_TILE, P_KEYS), 1)
            bias[...] = jnp.where(
                col < P_SPAN,
                jnp.where((col <= row) & (col > row - window), 0.0, HIDDEN),
                jnp.where(col - P_SPAN < n_sink, 0.0, HIDDEN),
            )

            @pl.when(t == 0)
            def _():
                for copy in copies + load_sinks(own) + queries:
                    copy.wait()

            rows = pl.ds(pl.multiple_of(t * P_TILE, P_TILE), P_SPAN)
            kt[0:P_SPAN, :] = kbuf[rows, :]
            vt[0:P_SPAN, 0:DH] = vbuf[rows, :]
            places = pl.ds(t * (P_TILE // TOK), P_TILE // TOK)

            def scores(i):
                qi = qbuf[places, :, i * DH : (i + 1) * DH].reshape(P_TILE, DH)
                return lax.dot_general(qi, kt[...], NT, preferred_element_type=f32)

            s_now = scores(0)
            for i in range(GROUP):
                ahead = scores(i + 1) if i + 1 < GROUP else None
                s_now = s_now + bias[...]
                top = jnp.max(s_now, -1, keepdims=True)
                p = jnp.exp2(s_now * LOG2E_SCALED - top * LOG2E_SCALED).astype(bf16)
                acc = jnp.dot(p, vt[...], preferred_element_type=f32)
                o = (acc[:, 0:DH] / acc[:, DH:]).astype(bf16)
                obuf[places, :, i * DH : (i + 1) * DH] = o.reshape(P_TILE // TOK, TOK, DH)
                give(t, i).start()
                s_now = ahead
            return 0

        lax.fori_loop(0, tiles, tile, 0)
        for t in range(tiles):
            for i in range(GROUP):
                give(t, i).wait()


R_CHUNK = 768
R_KEYS = 3 * R_CHUNK
R_QUERIES = 2 * PIECE


def retrieval_kernel(phase, place, *refs):
    if phase == 0:
        (*rings, column, across), (acc, top, qbuf), (kbuf, vbuf, sems, bias, ring_sems) = refs[:6], refs[6:9], refs[9:]
        chunks = column, across
    elif phase == 1:
        (*chunks, qbuf, old_acc, old_top), (acc, top), (kbuf, vbuf, sems) = refs[:6], refs[6:8], refs[8:]
    else:
        (*chunks, qbuf, old_acc, old_top), (out,), (kbuf, vbuf, sems, acc, top, obuf, out_sems) = refs[:6], refs[6:7], refs[7:]
    s, h = place[0], place[1]
    part = h % KEY_PARTS
    y, zh, core = s // 4, (s // 2) % 2, s % 2
    diagonal = R_NEW if phase == 0 else 0
    kbuf[R_CHUNK:, :] = jnp.zeros((R_KEYS - R_CHUNK, DH), bf16)
    vbuf[R_CHUNK:, 0:DH] = jnp.zeros((R_KEYS - R_CHUNK, DH), bf16)
    vbuf[:, DH:] = jnp.ones((R_KEYS, DH), bf16)

    def fetch(chunk, base, to, rows, sem):
        return [
            pltpu.make_async_copy(chunk.at[base : base + rows, 0:DH], kbuf.at[pl.ds(to, rows)], sems.at[sem]),
            pltpu.make_async_copy(
                chunk.at[base : base + rows, DH : 2 * DH], vbuf.at[pl.ds(to, rows), 0:DH], sems.at[sem + 1]
            ),
        ]

    at_once, later = [], []
    for i, chunk in enumerate(chunks):
        for dz in range(2):
            their_zh = zh if dz == 0 else 1 - zh
            if phase == 0:
                slot = 2 * their_zh + (core if i == 0 else 1 - core)
                seen = slot < s % 4
            else:
                their_y = (y + 3 - i) % 4
                slot = 2 * their_y + their_zh
                seen = their_y < y
            base = dz * R_ROWS
            sem = 4 * (2 * i + dz)
            at_once += fetch(chunk, base, diagonal + (2 * i + dz) * R_PRE, R_PRE, sem)
            if phase == 0 and i == 0 and dz == 0:
                at_once += fetch(chunk, base + R_PRE, 0, R_NEW, sem + 2)
            else:
                to = pl.multiple_of(R_CHUNK + slot * R_NEW, R_NEW)
                later.append((seen, fetch(chunk, base + R_PRE, to, R_NEW, sem + 2)))
    if phase == 0:
        for k, ring in enumerate(rings):
            x = (h + RING - k) % RING
            for i in range(GROUP):
                to = pl.ds(pl.multiple_of((i % 2) * PIECE + x * TOK, TOK), TOK)
                at_once.append(
                    pltpu.make_async_copy(
                        ring.at[:, i * DH : (i + 1) * DH], qbuf.at[i // 2, to], ring_sems.at[k * GROUP + i]
                    )
                )
    for copy in at_once:
        copy.start()
    for seen, copies in later:

        @pl.when(seen)
        def _():
            for copy in copies:
                copy.start()

    count = R_CHUNK + (s % 4 if phase == 0 else 2 * y) * R_NEW
    if phase == 0:
        token = lax.broadcasted_iota(jnp.int32, (R_QUERIES, R_NEW), 0) % PIECE + (h // RING) * PIECE
        col = lax.broadcasted_iota(jnp.int32, (R_QUERIES, R_NEW), 1)
        key = (col // R_NEW_DEV) * TOK + part * R_NEW_DEV + col % R_NEW_DEV
        bias[...] = jnp.where(key <= token, 0.0, HIDDEN)

    def scores(i, keys):
        return lax.dot_general(qbuf[i], keys, NT, preferred_element_type=f32)

    def step(j, kind):
        if kind in ("diagonal", "first"):
            rows = slice(0, R_CHUNK)
        else:
            rows = pl.ds(pl.multiple_of(j * R_CHUNK, R_CHUNK), R_CHUNK)
        keys = kbuf[rows, :]
        values = vbuf[rows, :]
        before, above = (old_acc, old_top) if kind == "first" else (acc, top)
        if kind == "last":
            at = lax.broadcasted_iota(jnp.int32, (1, R_CHUNK), 1) + j * R_CHUNK
            tail = jnp.where(at < count, 0.0, HIDDEN)
        s_now = scores(0, keys)
        for i in range(R_UNITS):
            ahead = scores(i + 1, keys) if i + 1 < R_UNITS else None
            if kind == "diagonal":
                s_now = jnp.concatenate([s_now[:, 0:R_NEW] + bias[...], s_now[:, R_NEW:]], 1)
            if kind == "last":
                s_now = s_now + tail
            fresh = jnp.broadcast_to(jnp.max(s_now, -1, keepdims=True), (R_QUERIES, DH))
            if kind != "diagonal":
                old = above[i]
                fresh = jnp.maximum(old, fresh)
                shrink = jnp.exp2((old - fresh) * LOG2E_SCALED)
            shift = jnp.concatenate([fresh * LOG2E_SCALED] * (R_CHUNK // DH), 1)
            p = jnp.exp2(s_now * LOG2E_SCALED - shift).astype(bf16)
            d = jnp.dot(p, values, preferred_element_type=f32)
            if kind != "diagonal":
                d = before[i] * jnp.concatenate([shrink, shrink], 1) + d
            top[i] = fresh
            acc[i] = d
            s_now = ahead

    def middle(j, _):
        step(j, "middle")
        return 0

    for copy in at_once:
        copy.wait()
    step(0, "diagonal" if phase == 0 else "first")
    for seen, copies in later:

        @pl.when(seen)
        def _():
            for copy in copies:
                copy.wait()

    lax.fori_loop(1, count // R_CHUNK, middle, 0)

    @pl.when(count % R_CHUNK > 0)
    def _():
        step(count // R_CHUNK, "last")

    if phase < 2:
        return

    lane = lax.broadcasted_iota(jnp.int32, (PIECE, DH), 1)
    logs = jnp.zeros((PIECE, DH), f32)
    copies = []

    def give(i):
        cols = slice(i * DH, (i + 1) * DH)
        copies.append(pltpu.make_async_copy(obuf.at[:, :, cols], out.at[:, :, cols], out_sems.at[i]))
        copies[-1].start()

    for i in range(GROUP):
        rows = slice((i % 2) * PIECE, (i % 2 + 1) * PIECE)
        total = acc[i // 2, rows, DH:]
        o = (acc[i // 2, rows, 0:DH] / total).astype(bf16)
        obuf[:, :, i * DH : (i + 1) * DH] = o.reshape(RING, TOK, DH)
        give(i)
        log = top[i // 2, rows] * LOG2E_SCALED + jnp.log2(total)
        hi = log.astype(bf16).astype(f32)
        mid = (log - hi).astype(bf16).astype(f32)
        lo = log - hi - mid
        logs = jnp.where(lane == 3 * i, hi, logs)
        logs = jnp.where(lane == 3 * i + 1, mid, logs)
        logs = jnp.where(lane == 3 * i + 2, lo, logs)
    obuf[:, :, WIDE:] = logs.astype(bf16).reshape(RING, TOK, DH)
    give(GROUP)
    for copy in copies:
        copy.wait()


def merge_kernel(partial, out):
    for which in range(2):
        pieces = [partial[which * KEY_PARTS + kp] for kp in range(KEY_PARTS)]
        logs3 = [piece[:, WIDE:].astype(f32) for piece in pieces]
        for i in range(GROUP):
            logs = [
                l[:, 3 * i : 3 * i + 1] + l[:, 3 * i + 1 : 3 * i + 2] + l[:, 3 * i + 2 : 3 * i + 3] for l in logs3
            ]
            top = functools.reduce(jnp.maximum, logs)
            shares = [jnp.exp2(x - top) for x in logs]
            total = functools.reduce(jnp.add, shares)
            o = sum(
                piece[:, i * DH : (i + 1) * DH].astype(f32) * (share / total)
                for piece, share in zip(pieces, shares)
            )
            out[which, :, i * DH : (i + 1) * DH] = o.astype(bf16)


COLUMNS_A_STEP = 2


def finish_kernel(flags, passing, merged, out):
    low, _ = retrieval_groups(flags)
    for j in range(COLUMNS_A_STEP):
        g = pl.program_id(0) * COLUMNS_A_STEP + j
        cols = slice(j * WIDE, (j + 1) * WIDE)

        @pl.when(flags[g] == 0)
        def _():
            out[:, cols] = passing[j]

        @pl.when(flags[g] == 1)
        def _():
            out[:, cols] = merged[jnp.where(g == low, 0, 1)]


def swap(x, axis):
    return lax.all_to_all(x, axis, split_axis=0, concat_axis=0, tiled=True)


def body(queries, new_keys, new_values, cache_keys, cache_values, retrieval, sinks, windows):
    column_index = lax.axis_index("zl") * RING + lax.axis_index("x")
    place = jnp.stack([lax.axis_index("seq"), column_index]).astype(jnp.int32)

    def send(x, pairs):
        return lax.ppermute(x, "seq", pairs)

    sds = jax.ShapeDtypeStruct
    two = 2 * DH
    packed, cache = call(
        pack_kv_kernel,
        (sds((HEAD, TOK + R_SEND, two), bf16), sds((PRE, two), bf16)),
        (retrieval, new_keys, new_values, cache_keys, cache_values),
        vmem=60,
    )
    got = swap(packed, ("zl", "x"))
    first = send(cache, [(10, 13), (12, 14), (14, 15), (0, 8)])
    second = send(cache, [(11, 13), (13, 14), (0, 4)])
    third = send(cache, [(0, 12)])
    ring = sds((TOK, WIDE), bf16)
    packed_q, *rings = call(
        pack_q_kernel,
        (sds((HEAD, TOK, WIDE), bf16), ring, ring, ring, ring),
        (retrieval, place, queries),
    )
    got, first, second, third, packed_q, *rings = lax.optimization_barrier(
        (got, first, second, third, packed_q, *rings)
    )
    rows = sds((CARRY, two), bf16)
    part, own, two_on, odd_on, even_on = call(
        unpack_kv_kernel,
        (sds((R_ROWS, two), bf16), rows, rows, rows, rows),
        (retrieval, place, got, cache, first, second, third),
    )
    cells = [(y, zh, c) for y in range(4) for zh in range(2) for c in range(2)]
    part, *rings = lax.optimization_barrier((part, *rings))
    back_z = send(part, [(4 * y + 2 * z + c, 4 * y + 2 * (1 - z) + c) for y, z, c in cells])
    rings = rings[:1] + [
        lax.ppermute(rings[k], "x", [(i, (i + k) % RING) for i in range(RING)]) for k in (1, 2, 3)
    ]
    column = jnp.concatenate([part, back_z], 0)
    column, packed_q = lax.optimization_barrier((column, packed_q))
    q = swap(packed_q, ("zl", "x"))
    own_core = [column] + [send(column, [(i, (i + 4 * k) % SEQ) for i in range(SEQ)]) for k in (1, 2, 3)]
    def other_core(x):
        return send(x, [(i, i ^ 1) for i in range(SEQ)])

    across = other_core(column)
    state = (
        sds((R_UNITS, R_QUERIES, 2 * DH), f32),
        sds((R_UNITS, R_QUERIES, DH), f32),
        sds((R_UNITS, R_QUERIES, DH), bf16),
    )
    dma = pltpu.SemaphoreType.DMA
    buffers = [
        pltpu.VMEM((R_KEYS, DH), bf16),
        pltpu.VMEM((R_KEYS, 2 * DH), bf16),
        dma((24,)),
    ]
    flops = R_UNITS * R_QUERIES * R_KEYS * 4 * DH
    acc, top, queried = call(
        functools.partial(retrieval_kernel, 0),
        state,
        (place, *rings, column, across),
        flops=flops,
        nbytes=2**22,
        scratch=buffers + [pltpu.VMEM((R_QUERIES, R_NEW), f32), dma((RING * GROUP,))],
        vmem=24,
        by_hand=True,
        resident=state,
    )
    same = own_core[1:]
    acc, two_on, odd_on, even_on, *same = lax.optimization_barrier((acc, two_on, odd_on, even_on, *same))
    other = [other_core(x) for x in same]
    back_two = send(two_on, [(i, (i + 2) % SEQ) for i in range(SEQ)])
    near = send(odd_on, [(i, (i + 1 + 2 * (i % 2)) % SEQ) for i in range(SEQ)])
    far = send(even_on, [(i, (i + 3 - 2 * (i % 2)) % SEQ) for i in range(SEQ)])
    acc, top = call(
        functools.partial(retrieval_kernel, 1),
        state[:2],
        (place, *same, queried, acc, top),
        flops=flops,
        nbytes=2**22,
        scratch=buffers,
        vmem=24,
        by_hand=True,
        resident=(*state, queried, acc, top),
    )
    acc, top, *other = lax.optimization_barrier((acc, top, *other))
    partial = call(
        functools.partial(retrieval_kernel, 2),
        sds((RING, TOK, R_LANES), bf16),
        (place, *other, queried, acc, top),
        flops=flops,
        nbytes=2**22,
        scratch=buffers
        + [pltpu.VMEM(a.shape, f32) for a in state[:2]]
        + [pltpu.VMEM((RING, TOK, R_LANES), bf16), dma((GROUP + 1,))],
        vmem=24,
        by_hand=True,
        resident=(queried, acc, top),
    )
    partial, q, far, near, back_two = lax.optimization_barrier((partial, q, far, near, back_two))
    partial_back = swap(partial, "x")
    passing = call(
        passing_kernel,
        sds((HEAD, TOK, WIDE), bf16),
        (place, retrieval, sinks, windows, q, far, back_two, near, own),
        flops=BLOCK * GROUP * P_KEYS * 4 * DH,
        nbytes=2**22,
        scratch=[
            pltpu.VMEM((4 * BLOCK, DH), bf16),
            pltpu.VMEM((4 * BLOCK, DH), bf16),
            pltpu.VMEM((P_KEYS, DH), bf16),
            pltpu.VMEM((P_KEYS, 2 * DH), bf16),
            pltpu.VMEM((HEAD, TOK, WIDE), bf16),
            pltpu.VMEM((HEAD, TOK, WIDE), bf16),
            pltpu.VMEM((P_TILE, P_KEYS), f32),
            dma((10,)),
            dma((GROUP,)),
            dma((BLOCK // P_TILE, GROUP)),
        ],
        vmem=58,
        by_hand=True,
    )
    passing, partial_back = lax.optimization_barrier((passing, partial_back))
    passing_back = swap(passing, ("zl", "x"))
    merged = call(merge_kernel, sds((2, TOK, WIDE), bf16), (partial_back,))
    return pl.pallas_call(
        finish_kernel,
        grid=(KVH // COLUMNS_A_STEP,),
        out_shape=sds((TOK, HQ * DH), bf16),
        in_specs=[
            SMEM,
            pl.BlockSpec((COLUMNS_A_STEP, TOK, WIDE), lambda i: (i, 0, 0)),
            pl.BlockSpec((2, TOK, WIDE), lambda i: (0, 0, 0)),
        ],
        out_specs=pl.BlockSpec((TOK, COLUMNS_A_STEP * WIDE), lambda i: (0, i)),
        compiler_params=pltpu.CompilerParams(vmem_limit_bytes=24 * 2**20),
    )(retrieval, passing_back, merged)


def solution(mesh):
    cut = jax.sharding.Mesh(mesh.devices.reshape(SEQ, 2, RING), ("seq", "zl", "x"))
    tokens = P(("seq", "zl", "x"), None)
    cache = P("seq", ("zl", "x"))
    return jax.shard_map(
        body,
        mesh=cut,
        in_specs=(tokens, tokens, tokens, cache, cache, P(), P(), P()),
        out_specs=tokens,
        check_vma=False,
    )
```

```python
import functools
import math

import jax
import jax.numpy as jnp
from jax import lax
from jax.experimental import pallas as pl
from jax.experimental.pallas import tpu as pltpu
from jax.sharding import PartitionSpec as P

HQ = 64
KVH = 8
DH = 128
GROUP = HQ // KVH
WIDE = GROUP * DH
SINKS = 64

SEQ, HEAD = 16, 8
TOK = 64
BLOCK = TOK * HEAD
PRE = 256
CARRY = BLOCK + SINKS
WINDOW_BLOCKS = 3

RING = 4
KEY_PARTS = 2
PIECE = TOK * RING
R_NEW_DEV = TOK // KEY_PARTS
R_NEW = BLOCK // KEY_PARTS
R_PRE = PRE // KEY_PARTS
R_SEND = R_NEW_DEV + R_PRE
R_ROWS = R_NEW + R_PRE
R_UNITS = 4
R_LANES = WIDE + DH

LOG2E_SCALED = math.log2(math.e) / math.sqrt(DH)
HIDDEN = -1e30
NT = (((1,), (1,)), ((), ()))

SMEM = pl.BlockSpec(memory_space=pltpu.SMEM)
bf16 = jnp.bfloat16
f32 = jnp.float32


VMEM = pl.BlockSpec(memory_space=pltpu.VMEM)
ANY = pl.BlockSpec(memory_space=pl.ANY)


def call(kernel, outs, ins, flops=0, nbytes=2**20, scratch=(), vmem=24, by_hand=False, resident=()):
    def spec(a, kept):
        if a.dtype == jnp.int32:
            return SMEM
        if kept:
            return VMEM
        return ANY if by_hand else pl.BlockSpec(a.shape, lambda i: (0,) * len(a.shape))

    listed = outs if isinstance(outs, (tuple, list)) else (outs,)
    kept_in = [any(a is r for r in resident) for a in ins]
    kept_out = [any(a is r for r in resident) for a in listed]
    return pl.pallas_call(
        kernel,
        grid=(1,),
        out_shape=outs,
        in_specs=[spec(a, k) for a, k in zip(ins, kept_in)],
        out_specs=jax.tree.unflatten(jax.tree.structure(outs), [spec(a, k) for a, k in zip(listed, kept_out)]),
        scratch_shapes=list(scratch),
        compiler_params=pltpu.CompilerParams(vmem_limit_bytes=vmem * 2**20),
        cost_estimate=pl.CostEstimate(flops=flops, bytes_accessed=nbytes, transcendentals=0),
    )(*ins)


def retrieval_groups(flags):
    low = jnp.int32(0)
    high = jnp.int32(0)
    for g in range(KVH):
        high = jnp.where(flags[g] == 1, g, high)
        low = jnp.where(flags[KVH - 1 - g] == 1, KVH - 1 - g, low)
    return low, high


def pack_kv_kernel(flags, nk, nv, ck, cv, out, cache):
    groups = retrieval_groups(flags)
    cache[:, 0:DH] = ck[...]
    cache[:, DH:] = cv[...]
    for h in range(HEAD):
        out[h, 0:TOK, 0:DH] = nk[:, h * DH : (h + 1) * DH]
        out[h, 0:TOK, DH:] = nv[:, h * DH : (h + 1) * DH]
        x = h % RING
        cols = pl.ds(pl.multiple_of(groups[x // KEY_PARTS] * DH, DH), DH)
        part = x % KEY_PARTS
        rows = slice(part * R_NEW_DEV, (part + 1) * R_NEW_DEV)
        end = TOK + R_NEW_DEV
        out[h, TOK:end, 0:DH] = nk[rows, cols]
        out[h, TOK:end, DH:] = nv[rows, cols]
        rows = slice(part * R_PRE, (part + 1) * R_PRE)
        out[h, end:, 0:DH] = ck[rows, :]
        out[h, end:, DH:] = cv[rows, :]


def unpack_kv_kernel(flags, place, got, cache, first, second, third, part, own, two_on, odd_on, even_on):
    s = place[0]
    low, high = retrieval_groups(flags)
    source = jnp.where((place[1] % RING) // KEY_PARTS == 0, low, high)
    end = TOK + R_NEW_DEV
    part[0:R_PRE, :] = got[source, end:, :]
    part[R_PRE:, :] = got[:, TOK:end, :].reshape(R_NEW, 2 * DH)
    whole = got[:, 0:TOK, :].reshape(BLOCK, 2 * DH)
    last = s == SEQ - 1
    sink = jnp.where(
        s == 0,
        cache[0:SINKS],
        jnp.where(s == 4, second[0:SINKS], jnp.where(s == 8, first[0:SINKS], third[0:SINKS])),
    )
    own[0:BLOCK, :] = whole
    own[BLOCK:, :] = sink
    odd = s % 2
    for shift, by in ((two_on, 2), (odd_on, 1 + 2 * odd), (even_on, 3 - 2 * odd)):
        shift[BLOCK:, :] = sink

        @pl.when(s + by < SEQ)
        def _():
            shift[0:BLOCK, :] = whole

        @pl.when(s + by >= SEQ)
        def _():
            shift[0:PRE, :] = first[...]
            shift[PRE:BLOCK, :] = jnp.where(last, cache[...], second[...])


def pack_q_kernel(flags, place, q, out, *rings):
    low, high = retrieval_groups(flags)
    for k, ring in enumerate(rings):
        other = (place[1] + k) % RING
        start = pl.multiple_of(jnp.where(other // KEY_PARTS == 0, low, high) * WIDE, WIDE)
        ring[...] = q[:, pl.ds(start, WIDE)]
    for h in range(HEAD):
        out[h] = q[:, h * WIDE : (h + 1) * WIDE]


P_TILE = 256
P_SPAN = WINDOW_BLOCKS * BLOCK + P_TILE
P_KEYS = P_SPAN + DH


def passing_kernel(place, flags, sinks, windows, q, far, two, near, own, out, kbuf, vbuf, kt, vt, qbuf, obuf, bias, kv_sems, q_sems, out_sems):
    s, h = place[0], place[1]
    odd = s % 2
    tiles = BLOCK // P_TILE

    @pl.when(flags[h] == 0)
    def _():
        n_sink, window = sinks[h], windows[h]

        def load(block, rows, sem):
            return [
                pltpu.make_async_copy(block.at[0:BLOCK, 0:DH], kbuf.at[rows], kv_sems.at[sem]),
                pltpu.make_async_copy(block.at[0:BLOCK, DH : 2 * DH], vbuf.at[rows], kv_sems.at[sem + 1]),
            ]

        copies = []
        for i, (at, block) in enumerate(((2 * odd, near), (1, two), (2 - 2 * odd, far), (3, own))):
            copies += load(block, pl.ds(pl.multiple_of(at * BLOCK, BLOCK), BLOCK), 2 * i)
        for copy in copies:
            copy.start()

        def load_sinks(block):
            rows = pl.ds(P_SPAN, SINKS)
            return [
                pltpu.make_async_copy(block.at[BLOCK:CARRY, 0:DH], kt.at[rows], kv_sems.at[8]),
                pltpu.make_async_copy(block.at[BLOCK:CARRY, DH : 2 * DH], vt.at[rows, 0:DH], kv_sems.at[9]),
            ]

        for i, block in enumerate((own, near, two, far)):

            @pl.when(s % 4 == i)
            def _():
                for copy in load_sinks(block):
                    copy.start()

        queries = []
        for i in range(GROUP):
            cols = slice(i * DH, (i + 1) * DH)
            queries.append(pltpu.make_async_copy(q.at[:, :, cols], qbuf.at[:, :, cols], q_sems.at[i]))
            queries[-1].start()
        kt[P_SPAN + SINKS :, :] = jnp.zeros((DH - SINKS, DH), bf16)
        vt[P_SPAN + SINKS :, 0:DH] = jnp.zeros((DH - SINKS, DH), bf16)
        vt[:, DH:] = jnp.ones((P_KEYS, DH), bf16)

        def give(t, i):
            places, cols = pl.ds(t * (P_TILE // TOK), P_TILE // TOK), slice(i * DH, (i + 1) * DH)
            return pltpu.make_async_copy(obuf.at[places, :, cols], out.at[places, :, cols], out_sems.at[t, i])

        def tile(t, _):
            row = lax.broadcasted_iota(jnp.int32, (P_TILE, P_KEYS), 0) + WINDOW_BLOCKS * BLOCK
            col = lax.broadcasted_iota(jnp.int32, (P_TILE, P_KEYS), 1)
            bias[...] = jnp.where(
                col < P_SPAN,
                jnp.where((col <= row) & (col > row - window), 0.0, HIDDEN),
                jnp.where(col - P_SPAN < n_sink, 0.0, HIDDEN),
            )

            @pl.when(t == 0)
            def _():
                for copy in copies + load_sinks(own) + queries:
                    copy.wait()

            rows = pl.ds(pl.multiple_of(t * P_TILE, P_TILE), P_SPAN)
            kt[0:P_SPAN, :] = kbuf[rows, :]
            vt[0:P_SPAN, 0:DH] = vbuf[rows, :]
            places = pl.ds(t * (P_TILE // TOK), P_TILE // TOK)

            def scores(i):
                qi = qbuf[places, :, i * DH : (i + 1) * DH].reshape(P_TILE, DH)
                return lax.dot_general(qi, kt[...], NT, preferred_element_type=f32)

            s_now = scores(0)
            for i in range(GROUP):
                ahead = scores(i + 1) if i + 1 < GROUP else None
                s_now = s_now + bias[...]
                top = jnp.max(s_now, -1, keepdims=True)
                p = jnp.exp2(s_now * LOG2E_SCALED - top * LOG2E_SCALED).astype(bf16)
                acc = jnp.dot(p, vt[...], preferred_element_type=f32)
                o = (acc[:, 0:DH] / acc[:, DH:]).astype(bf16)
                obuf[places, :, i * DH : (i + 1) * DH] = o.reshape(P_TILE // TOK, TOK, DH)
                give(t, i).start()
                s_now = ahead
            return 0

        lax.fori_loop(0, tiles, tile, 0)
        for t in range(tiles):
            for i in range(GROUP):
                give(t, i).wait()


R_CHUNK = 768
R_KEYS = 3 * R_CHUNK
R_QUERIES = 2 * PIECE


def retrieval_kernel(phase, place, *refs):
    if phase == 0:
        (*rings, column, across), (acc, top, qbuf), (kbuf, vbuf, sems, bias, ring_sems) = refs[:6], refs[6:9], refs[9:]
        chunks = column, across
    elif phase == 1:
        (*chunks, qbuf, old_acc, old_top), (acc, top), (kbuf, vbuf, sems) = refs[:6], refs[6:8], refs[8:]
    else:
        (*chunks, qbuf, old_acc, old_top), (out,), (kbuf, vbuf, sems, acc, top, obuf, out_sems) = refs[:6], refs[6:7], refs[7:]
    s, h = place[0], place[1]
    part = h % KEY_PARTS
    y, zh, core = s // 4, (s // 2) % 2, s % 2
    diagonal = R_NEW if phase == 0 else 0
    kbuf[R_CHUNK:, :] = jnp.zeros((R_KEYS - R_CHUNK, DH), bf16)
    vbuf[R_CHUNK:, 0:DH] = jnp.zeros((R_KEYS - R_CHUNK, DH), bf16)
    vbuf[:, DH:] = jnp.ones((R_KEYS, DH), bf16)

    def fetch(chunk, base, to, rows, sem):
        return [
            pltpu.make_async_copy(chunk.at[base : base + rows, 0:DH], kbuf.at[pl.ds(to, rows)], sems.at[sem]),
            pltpu.make_async_copy(
                chunk.at[base : base + rows, DH : 2 * DH], vbuf.at[pl.ds(to, rows), 0:DH], sems.at[sem + 1]
            ),
        ]

    at_once, later = [], []
    for i, chunk in enumerate(chunks):
        for dz in range(2):
            their_zh = zh if dz == 0 else 1 - zh
            if phase == 0:
                slot = 2 * their_zh + (core if i == 0 else 1 - core)
                seen = slot < s % 4
            else:
                their_y = (y + 3 - i) % 4
                slot = 2 * their_y + their_zh
                seen = their_y < y
            base = dz * R_ROWS
            sem = 4 * (2 * i + dz)
            at_once += fetch(chunk, base, diagonal + (2 * i + dz) * R_PRE, R_PRE, sem)
            if phase == 0 and i == 0 and dz == 0:
                at_once += fetch(chunk, base + R_PRE, 0, R_NEW, sem + 2)
            else:
                to = pl.multiple_of(R_CHUNK + slot * R_NEW, R_NEW)
                later.append((seen, fetch(chunk, base + R_PRE, to, R_NEW, sem + 2)))
    if phase == 0:
        for k, ring in enumerate(rings):
            x = (h + RING - k) % RING
            for i in range(GROUP):
                to = pl.ds(pl.multiple_of((i % 2) * PIECE + x * TOK, TOK), TOK)
                at_once.append(
                    pltpu.make_async_copy(
                        ring.at[:, i * DH : (i + 1) * DH], qbuf.at[i // 2, to], ring_sems.at[k * GROUP + i]
                    )
                )
    for copy in at_once:
        copy.start()
    for seen, copies in later:

        @pl.when(seen)
        def _():
            for copy in copies:
                copy.start()

    count = R_CHUNK + (s % 4 if phase == 0 else 2 * y) * R_NEW
    if phase == 0:
        token = lax.broadcasted_iota(jnp.int32, (R_QUERIES, R_NEW), 0) % PIECE + (h // RING) * PIECE
        col = lax.broadcasted_iota(jnp.int32, (R_QUERIES, R_NEW), 1)
        key = (col // R_NEW_DEV) * TOK + part * R_NEW_DEV + col % R_NEW_DEV
        bias[...] = jnp.where(key <= token, 0.0, HIDDEN)

    def scores(i, keys):
        return lax.dot_general(qbuf[i], keys, NT, preferred_element_type=f32)

    def step(j, kind):
        if kind in ("diagonal", "first"):
            rows = slice(0, R_CHUNK)
        else:
            rows = pl.ds(pl.multiple_of(j * R_CHUNK, R_CHUNK), R_CHUNK)
        keys = kbuf[rows, :]
        values = vbuf[rows, :]
        before, above = (old_acc, old_top) if kind == "first" else (acc, top)
        if kind == "later":
            at = lax.broadcasted_iota(jnp.int32, (1, R_CHUNK), 1) + j * R_CHUNK
            tail = jnp.where(at < count, 0.0, HIDDEN)
        s_now = scores(0, keys)
        for i in range(R_UNITS):
            ahead = scores(i + 1, keys) if i + 1 < R_UNITS else None
            if kind == "diagonal":
                s_now = jnp.concatenate([s_now[:, 0:R_NEW] + bias[...], s_now[:, R_NEW:]], 1)
            if kind == "later":
                s_now = s_now + tail
            fresh = jnp.broadcast_to(jnp.max(s_now, -1, keepdims=True), (R_QUERIES, DH))
            if kind != "diagonal":
                old = above[i]
                fresh = jnp.maximum(old, fresh)
                shrink = jnp.exp2((old - fresh) * LOG2E_SCALED)
            shift = jnp.concatenate([fresh * LOG2E_SCALED] * (R_CHUNK // DH), 1)
            p = jnp.exp2(s_now * LOG2E_SCALED - shift).astype(bf16)
            d = jnp.dot(p, values, preferred_element_type=f32)
            if kind != "diagonal":
                d = before[i] * jnp.concatenate([shrink, shrink], 1) + d
            top[i] = fresh
            acc[i] = d
            s_now = ahead

    def later_step(j, _):
        step(j, "later")
        return 0

    for copy in at_once:
        copy.wait()
    step(0, "diagonal" if phase == 0 else "first")
    for seen, copies in later:

        @pl.when(seen)
        def _():
            for copy in copies:
                copy.wait()

    lax.fori_loop(1, (count + R_CHUNK - 1) // R_CHUNK, later_step, 0)

    if phase < 2:
        return

    lane = lax.broadcasted_iota(jnp.int32, (PIECE, DH), 1)
    logs = jnp.zeros((PIECE, DH), f32)
    copies = []

    def give(i):
        cols = slice(i * DH, (i + 1) * DH)
        copies.append(pltpu.make_async_copy(obuf.at[:, :, cols], out.at[:, :, cols], out_sems.at[i]))
        copies[-1].start()

    for i in range(GROUP):
        rows = slice((i % 2) * PIECE, (i % 2 + 1) * PIECE)
        total = acc[i // 2, rows, DH:]
        o = (acc[i // 2, rows, 0:DH] / total).astype(bf16)
        obuf[:, :, i * DH : (i + 1) * DH] = o.reshape(RING, TOK, DH)
        give(i)
        log = top[i // 2, rows] * LOG2E_SCALED + jnp.log2(total)
        hi = log.astype(bf16).astype(f32)
        mid = (log - hi).astype(bf16).astype(f32)
        lo = log - hi - mid
        logs = jnp.where(lane == 3 * i, hi, logs)
        logs = jnp.where(lane == 3 * i + 1, mid, logs)
        logs = jnp.where(lane == 3 * i + 2, lo, logs)
    obuf[:, :, WIDE:] = logs.astype(bf16).reshape(RING, TOK, DH)
    give(GROUP)
    for copy in copies:
        copy.wait()


def merge_kernel(partial, out):
    for which in range(2):
        pieces = [partial[which * KEY_PARTS + kp] for kp in range(KEY_PARTS)]
        logs3 = [piece[:, WIDE:].astype(f32) for piece in pieces]
        for i in range(GROUP):
            logs = [
                l[:, 3 * i : 3 * i + 1] + l[:, 3 * i + 1 : 3 * i + 2] + l[:, 3 * i + 2 : 3 * i + 3] for l in logs3
            ]
            top = functools.reduce(jnp.maximum, logs)
            shares = [jnp.exp2(x - top) for x in logs]
            total = functools.reduce(jnp.add, shares)
            o = sum(
                piece[:, i * DH : (i + 1) * DH].astype(f32) * (share / total)
                for piece, share in zip(pieces, shares)
            )
            out[which, :, i * DH : (i + 1) * DH] = o.astype(bf16)


COLUMNS_A_STEP = 2


def finish_kernel(flags, passing, merged, out):
    low, _ = retrieval_groups(flags)
    for j in range(COLUMNS_A_STEP):
        g = pl.program_id(0) * COLUMNS_A_STEP + j
        cols = slice(j * WIDE, (j + 1) * WIDE)

        @pl.when(flags[g] == 0)
        def _():
            out[:, cols] = passing[j]

        @pl.when(flags[g] == 1)
        def _():
            out[:, cols] = merged[jnp.where(g == low, 0, 1)]


def swap(x, axis):
    return lax.all_to_all(x, axis, split_axis=0, concat_axis=0, tiled=True)


def body(queries, new_keys, new_values, cache_keys, cache_values, retrieval, sinks, windows):
    column_index = lax.axis_index("zl") * RING + lax.axis_index("x")
    place = jnp.stack([lax.axis_index("seq"), column_index]).astype(jnp.int32)

    def send(x, pairs):
        return lax.ppermute(x, "seq", pairs)

    sds = jax.ShapeDtypeStruct
    two = 2 * DH
    packed, cache = call(
        pack_kv_kernel,
        (sds((HEAD, TOK + R_SEND, two), bf16), sds((PRE, two), bf16)),
        (retrieval, new_keys, new_values, cache_keys, cache_values),
        vmem=60,
    )
    got = swap(packed, ("zl", "x"))
    first = send(cache, [(10, 13), (12, 14), (14, 15), (0, 8)])
    second = send(cache, [(11, 13), (13, 14), (0, 4)])
    third = send(cache, [(0, 12)])
    ring = sds((TOK, WIDE), bf16)
    packed_q, *rings = call(
        pack_q_kernel,
        (sds((HEAD, TOK, WIDE), bf16), ring, ring, ring, ring),
        (retrieval, place, queries),
    )
    got, first, second, third, packed_q, *rings = lax.optimization_barrier(
        (got, first, second, third, packed_q, *rings)
    )
    rows = sds((CARRY, two), bf16)
    part, own, two_on, odd_on, even_on = call(
        unpack_kv_kernel,
        (sds((R_ROWS, two), bf16), rows, rows, rows, rows),
        (retrieval, place, got, cache, first, second, third),
    )
    cells = [(y, zh, c) for y in range(4) for zh in range(2) for c in range(2)]
    part, *rings = lax.optimization_barrier((part, *rings))
    back_z = send(part, [(4 * y + 2 * z + c, 4 * y + 2 * (1 - z) + c) for y, z, c in cells])
    rings = rings[:1] + [
        lax.ppermute(rings[k], "x", [(i, (i + k) % RING) for i in range(RING)]) for k in (1, 2, 3)
    ]
    column = jnp.concatenate([part, back_z], 0)
    column, packed_q = lax.optimization_barrier((column, packed_q))
    q = swap(packed_q, ("zl", "x"))
    own_core = [column] + [send(column, [(i, (i + 4 * k) % SEQ) for i in range(SEQ)]) for k in (1, 2, 3)]
    def other_core(x):
        return send(x, [(i, i ^ 1) for i in range(SEQ)])

    across = other_core(column)
    state = (
        sds((R_UNITS, R_QUERIES, 2 * DH), f32),
        sds((R_UNITS, R_QUERIES, DH), f32),
        sds((R_UNITS, R_QUERIES, DH), bf16),
    )
    dma = pltpu.SemaphoreType.DMA
    buffers = [
        pltpu.VMEM((R_KEYS, DH), bf16),
        pltpu.VMEM((R_KEYS, 2 * DH), bf16),
        dma((24,)),
    ]
    flops = R_UNITS * R_QUERIES * R_KEYS * 4 * DH
    acc, top, queried = call(
        functools.partial(retrieval_kernel, 0),
        state,
        (place, *rings, column, across),
        flops=flops,
        nbytes=2**22,
        scratch=buffers + [pltpu.VMEM((R_QUERIES, R_NEW), f32), dma((RING * GROUP,))],
        vmem=24,
        by_hand=True,
        resident=state,
    )
    same = own_core[1:]
    acc, two_on, odd_on, even_on, *same = lax.optimization_barrier((acc, two_on, odd_on, even_on, *same))
    other = [other_core(x) for x in same]
    back_two = send(two_on, [(i, (i + 2) % SEQ) for i in range(SEQ)])
    near = send(odd_on, [(i, (i + 1 + 2 * (i % 2)) % SEQ) for i in range(SEQ)])
    far = send(even_on, [(i, (i + 3 - 2 * (i % 2)) % SEQ) for i in range(SEQ)])
    acc, top = call(
        functools.partial(retrieval_kernel, 1),
        state[:2],
        (place, *same, queried, acc, top),
        flops=flops,
        nbytes=2**22,
        scratch=buffers,
        vmem=24,
        by_hand=True,
        resident=(*state, queried, acc, top),
    )
    acc, top, *other = lax.optimization_barrier((acc, top, *other))
    partial = call(
        functools.partial(retrieval_kernel, 2),
        sds((RING, TOK, R_LANES), bf16),
        (place, *other, queried, acc, top),
        flops=flops,
        nbytes=2**22,
        scratch=buffers
        + [pltpu.VMEM(a.shape, f32) for a in state[:2]]
        + [pltpu.VMEM((RING, TOK, R_LANES), bf16), dma((GROUP + 1,))],
        vmem=24,
        by_hand=True,
        resident=(queried, acc, top),
    )
    partial, q, far, near, back_two = lax.optimization_barrier((partial, q, far, near, back_two))
    partial_back = swap(partial, "x")
    passing = call(
        passing_kernel,
        sds((HEAD, TOK, WIDE), bf16),
        (place, retrieval, sinks, windows, q, far, back_two, near, own),
        flops=BLOCK * GROUP * P_KEYS * 4 * DH,
        nbytes=2**22,
        scratch=[
            pltpu.VMEM((4 * BLOCK, DH), bf16),
            pltpu.VMEM((4 * BLOCK, DH), bf16),
            pltpu.VMEM((P_KEYS, DH), bf16),
            pltpu.VMEM((P_KEYS, 2 * DH), bf16),
            pltpu.VMEM((HEAD, TOK, WIDE), bf16),
            pltpu.VMEM((HEAD, TOK, WIDE), bf16),
            pltpu.VMEM((P_TILE, P_KEYS), f32),
            dma((10,)),
            dma((GROUP,)),
            dma((BLOCK // P_TILE, GROUP)),
        ],
        vmem=58,
        by_hand=True,
    )
    passing, partial_back = lax.optimization_barrier((passing, partial_back))
    passing_back = swap(passing, ("zl", "x"))
    merged = call(merge_kernel, sds((2, TOK, WIDE), bf16), (partial_back,))
    return pl.pallas_call(
        finish_kernel,
        grid=(KVH // COLUMNS_A_STEP,),
        out_shape=sds((TOK, HQ * DH), bf16),
        in_specs=[
            SMEM,
            pl.BlockSpec((COLUMNS_A_STEP, TOK, WIDE), lambda i: (i, 0, 0)),
            pl.BlockSpec((2, TOK, WIDE), lambda i: (0, 0, 0)),
        ],
        out_specs=pl.BlockSpec((TOK, COLUMNS_A_STEP * WIDE), lambda i: (0, i)),
        compiler_params=pltpu.CompilerParams(vmem_limit_bytes=24 * 2**20),
    )(retrieval, passing_back, merged)


def solution(mesh):
    cut = jax.sharding.Mesh(mesh.devices.reshape(SEQ, 2, RING), ("seq", "zl", "x"))
    tokens = P(("seq", "zl", "x"), None)
    cache = P("seq", ("zl", "x"))
    return jax.shard_map(
        body,
        mesh=cut,
        in_specs=(tokens, tokens, tokens, cache, cache, P(), P(), P()),
        out_specs=tokens,
        check_vma=False,
    )
```

```python
import functools
import math

import jax
import jax.numpy as jnp
from jax import lax
from jax.experimental import pallas as pl
from jax.experimental.pallas import tpu as pltpu
from jax.sharding import PartitionSpec as P

HQ = 64
KVH = 8
DH = 128
GROUP = HQ // KVH
WIDE = GROUP * DH
SINKS = 64

SEQ, HEAD = 16, 8
TOK = 64
BLOCK = TOK * HEAD
PRE = 256
CARRY = BLOCK + SINKS
WINDOW_BLOCKS = 3

RING = 4
KEY_PARTS = 2
PIECE = TOK * RING
R_NEW_DEV = TOK // KEY_PARTS
R_NEW = BLOCK // KEY_PARTS
R_PRE = PRE // KEY_PARTS
R_SEND = R_NEW_DEV + R_PRE
R_ROWS = R_NEW + R_PRE
R_UNITS = 4
R_LANES = WIDE + DH

LOG2E_SCALED = math.log2(math.e) / math.sqrt(DH)
HIDDEN = -1e30
NT = (((1,), (1,)), ((), ()))

SMEM = pl.BlockSpec(memory_space=pltpu.SMEM)
bf16 = jnp.bfloat16
f32 = jnp.float32


VMEM = pl.BlockSpec(memory_space=pltpu.VMEM)
ANY = pl.BlockSpec(memory_space=pl.ANY)


def call(kernel, outs, ins, flops=0, nbytes=2**20, scratch=(), vmem=24, by_hand=False, resident=()):
    def spec(a, kept):
        if a.dtype == jnp.int32:
            return SMEM
        if kept:
            return VMEM
        return ANY if by_hand else pl.BlockSpec(a.shape, lambda i: (0,) * len(a.shape))

    listed = outs if isinstance(outs, (tuple, list)) else (outs,)
    kept_in = [any(a is r for r in resident) for a in ins]
    kept_out = [any(a is r for r in resident) for a in listed]
    return pl.pallas_call(
        kernel,
        grid=(1,),
        out_shape=outs,
        in_specs=[spec(a, k) for a, k in zip(ins, kept_in)],
        out_specs=jax.tree.unflatten(jax.tree.structure(outs), [spec(a, k) for a, k in zip(listed, kept_out)]),
        scratch_shapes=list(scratch),
        compiler_params=pltpu.CompilerParams(vmem_limit_bytes=vmem * 2**20),
        cost_estimate=pl.CostEstimate(flops=flops, bytes_accessed=nbytes, transcendentals=0),
    )(*ins)


def retrieval_groups(flags):
    low = jnp.int32(0)
    high = jnp.int32(0)
    for g in range(KVH):
        high = jnp.where(flags[g] == 1, g, high)
        low = jnp.where(flags[KVH - 1 - g] == 1, KVH - 1 - g, low)
    return low, high


def pack_kv_kernel(flags, nk, nv, ck, cv, out, cache):
    groups = retrieval_groups(flags)
    cache[:, 0:DH] = ck[...]
    cache[:, DH:] = cv[...]
    for h in range(HEAD):
        out[h, 0:TOK, 0:DH] = nk[:, h * DH : (h + 1) * DH]
        out[h, 0:TOK, DH:] = nv[:, h * DH : (h + 1) * DH]
        x = h % RING
        cols = pl.ds(pl.multiple_of(groups[x // KEY_PARTS] * DH, DH), DH)
        part = x % KEY_PARTS
        rows = slice(part * R_NEW_DEV, (part + 1) * R_NEW_DEV)
        end = TOK + R_NEW_DEV
        out[h, TOK:end, 0:DH] = nk[rows, cols]
        out[h, TOK:end, DH:] = nv[rows, cols]
        rows = slice(part * R_PRE, (part + 1) * R_PRE)
        out[h, end:, 0:DH] = ck[rows, :]
        out[h, end:, DH:] = cv[rows, :]


def unpack_kv_kernel(flags, place, got, cache, first, second, third, part, own, two_on, odd_on):
    s = place[0]
    low, high = retrieval_groups(flags)
    source = jnp.where((place[1] % RING) // KEY_PARTS == 0, low, high)
    end = TOK + R_NEW_DEV
    part[0:R_PRE, :] = got[source, end:, :]
    part[R_PRE:, :] = got[:, TOK:end, :].reshape(R_NEW, 2 * DH)
    whole = got[:, 0:TOK, :].reshape(BLOCK, 2 * DH)
    last = s == SEQ - 1
    sink = jnp.where(
        s == 0,
        cache[0:SINKS],
        jnp.where(s == 4, second[0:SINKS], jnp.where(s == 8, first[0:SINKS], third[0:SINKS])),
    )
    own[0:BLOCK, :] = whole
    own[BLOCK:, :] = sink
    odd = s % 2
    for shift, by in ((two_on, 2), (odd_on, 1 + 2 * odd)):
        shift[BLOCK:, :] = sink

        @pl.when(s + by < SEQ)
        def _():
            shift[0:BLOCK, :] = whole

        @pl.when(s + by >= SEQ)
        def _():
            shift[0:PRE, :] = first[...]
            shift[PRE:BLOCK, :] = jnp.where(last, cache[...], second[...])


def pack_q_kernel(flags, place, q, out, *rings):
    low, high = retrieval_groups(flags)
    for k, ring in enumerate(rings):
        other = (place[1] + k) % RING
        start = pl.multiple_of(jnp.where(other // KEY_PARTS == 0, low, high) * WIDE, WIDE)
        ring[...] = q[:, pl.ds(start, WIDE)]
    for h in range(HEAD):
        out[h] = q[:, h * WIDE : (h + 1) * WIDE]


P_TILE = 256
P_SPAN = WINDOW_BLOCKS * BLOCK + P_TILE
P_KEYS = P_SPAN + DH


def passing_kernel(place, flags, sinks, windows, q, far, two, near, own, out, kbuf, vbuf, kt, vt, qbuf, obuf, bias, kv_sems, q_sems, out_sems):
    s, h = place[0], place[1]
    odd = s % 2
    tiles = BLOCK // P_TILE

    @pl.when(flags[h] == 0)
    def _():
        n_sink, window = sinks[h], windows[h]

        def load(block, rows, sem):
            return [
                pltpu.make_async_copy(block.at[0:BLOCK, 0:DH], kbuf.at[rows], kv_sems.at[sem]),
                pltpu.make_async_copy(block.at[0:BLOCK, DH : 2 * DH], vbuf.at[rows], kv_sems.at[sem + 1]),
            ]

        copies = []
        for i, (at, block) in enumerate(((2 * odd, near), (1, two), (2 - 2 * odd, far), (3, own))):
            copies += load(block, pl.ds(pl.multiple_of(at * BLOCK, BLOCK), BLOCK), 2 * i)
        for copy in copies:
            copy.start()

        def load_sinks(block):
            rows = pl.ds(P_SPAN, SINKS)
            return [
                pltpu.make_async_copy(block.at[BLOCK:CARRY, 0:DH], kt.at[rows], kv_sems.at[8]),
                pltpu.make_async_copy(block.at[BLOCK:CARRY, DH : 2 * DH], vt.at[rows, 0:DH], kv_sems.at[9]),
            ]

        for i, block in enumerate((own, near, two, far)):

            @pl.when(s % 4 == i)
            def _():
                for copy in load_sinks(block):
                    copy.start()

        queries = []
        for i in range(GROUP):
            cols = slice(i * DH, (i + 1) * DH)
            queries.append(pltpu.make_async_copy(q.at[:, :, cols], qbuf.at[:, :, cols], q_sems.at[i]))
            queries[-1].start()
        kt[P_SPAN + SINKS :, :] = jnp.zeros((DH - SINKS, DH), bf16)
        vt[P_SPAN + SINKS :, 0:DH] = jnp.zeros((DH - SINKS, DH), bf16)
        vt[:, DH:] = jnp.ones((P_KEYS, DH), bf16)

        def give(t, i):
            places, cols = pl.ds(t * (P_TILE // TOK), P_TILE // TOK), slice(i * DH, (i + 1) * DH)
            return pltpu.make_async_copy(obuf.at[places, :, cols], out.at[places, :, cols], out_sems.at[t, i])

        def tile(t, _):
            row = lax.broadcasted_iota(jnp.int32, (P_TILE, P_KEYS), 0) + WINDOW_BLOCKS * BLOCK
            col = lax.broadcasted_iota(jnp.int32, (P_TILE, P_KEYS), 1)
            bias[...] = jnp.where(
                col < P_SPAN,
                jnp.where((col <= row) & (col > row - window), 0.0, HIDDEN),
                jnp.where(col - P_SPAN < n_sink, 0.0, HIDDEN),
            )

            @pl.when(t == 0)
            def _():
                for copy in copies + load_sinks(own) + queries:
                    copy.wait()

            rows = pl.ds(pl.multiple_of(t * P_TILE, P_TILE), P_SPAN)
            kt[0:P_SPAN, :] = kbuf[rows, :]
            vt[0:P_SPAN, 0:DH] = vbuf[rows, :]
            places = pl.ds(t * (P_TILE // TOK), P_TILE // TOK)

            def scores(i):
                qi = qbuf[places, :, i * DH : (i + 1) * DH].reshape(P_TILE, DH)
                return lax.dot_general(qi, kt[...], NT, preferred_element_type=f32)

            s_now = scores(0)
            for i in range(GROUP):
                ahead = scores(i + 1) if i + 1 < GROUP else None
                s_now = s_now + bias[...]
                top = jnp.max(s_now, -1, keepdims=True)
                p = jnp.exp2(s_now * LOG2E_SCALED - top * LOG2E_SCALED).astype(bf16)
                acc = jnp.dot(p, vt[...], preferred_element_type=f32)
                o = (acc[:, 0:DH] / acc[:, DH:]).astype(bf16)
                obuf[places, :, i * DH : (i + 1) * DH] = o.reshape(P_TILE // TOK, TOK, DH)
                give(t, i).start()
                s_now = ahead
            return 0

        lax.fori_loop(0, tiles, tile, 0)
        for t in range(tiles):
            for i in range(GROUP):
                give(t, i).wait()


R_CHUNK = 768
R_KEYS = 3 * R_CHUNK
R_QUERIES = 2 * PIECE


def retrieval_kernel(phase, place, *refs):
    if phase == 0:
        (*rings, column, across), (acc, top, qbuf), (kbuf, vbuf, sems, bias, ring_sems) = refs[:6], refs[6:9], refs[9:]
        chunks = column, across
    elif phase == 1:
        (*chunks, qbuf, old_acc, old_top), (acc, top), (kbuf, vbuf, sems) = refs[:6], refs[6:8], refs[8:]
    else:
        (*chunks, qbuf, old_acc, old_top), (out,), (kbuf, vbuf, sems, acc, top, obuf, out_sems) = refs[:6], refs[6:7], refs[7:]
    s, h = place[0], place[1]
    part = h % KEY_PARTS
    y, zh, core = s // 4, (s // 2) % 2, s % 2
    diagonal = R_NEW if phase == 0 else 0
    kbuf[R_CHUNK:, :] = jnp.zeros((R_KEYS - R_CHUNK, DH), bf16)
    vbuf[R_CHUNK:, 0:DH] = jnp.zeros((R_KEYS - R_CHUNK, DH), bf16)
    vbuf[:, DH:] = jnp.ones((R_KEYS, DH), bf16)

    def fetch(chunk, base, to, rows, sem):
        return [
            pltpu.make_async_copy(chunk.at[base : base + rows, 0:DH], kbuf.at[pl.ds(to, rows)], sems.at[sem]),
            pltpu.make_async_copy(
                chunk.at[base : base + rows, DH : 2 * DH], vbuf.at[pl.ds(to, rows), 0:DH], sems.at[sem + 1]
            ),
        ]

    at_once, later = [], []
    for i, chunk in enumerate(chunks):
        for dz in range(2):
            their_zh = zh if dz == 0 else 1 - zh
            if phase == 0:
                slot = 2 * their_zh + (core if i == 0 else 1 - core)
                seen = slot < s % 4
            else:
                their_y = (y + 3 - i) % 4
                slot = 2 * their_y + their_zh
                seen = their_y < y
            base = dz * R_ROWS
            sem = 4 * (2 * i + dz)
            at_once += fetch(chunk, base, diagonal + (2 * i + dz) * R_PRE, R_PRE, sem)
            if phase == 0 and i == 0 and dz == 0:
                at_once += fetch(chunk, base + R_PRE, 0, R_NEW, sem + 2)
            else:
                to = pl.multiple_of(R_CHUNK + slot * R_NEW, R_NEW)
                later.append((seen, fetch(chunk, base + R_PRE, to, R_NEW, sem + 2)))
    if phase == 0:
        for k, ring in enumerate(rings):
            x = (h + RING - k) % RING
            for i in range(GROUP):
                to = pl.ds(pl.multiple_of((i % 2) * PIECE + x * TOK, TOK), TOK)
                at_once.append(
                    pltpu.make_async_copy(
                        ring.at[:, i * DH : (i + 1) * DH], qbuf.at[i // 2, to], ring_sems.at[k * GROUP + i]
                    )
                )
    for copy in at_once:
        copy.start()
    for seen, copies in later:

        @pl.when(seen)
        def _():
            for copy in copies:
                copy.start()

    count = R_CHUNK + (s % 4 if phase == 0 else 2 * y) * R_NEW
    if phase == 0:
        token = lax.broadcasted_iota(jnp.int32, (R_QUERIES, R_NEW), 0) % PIECE + (h // RING) * PIECE
        col = lax.broadcasted_iota(jnp.int32, (R_QUERIES, R_NEW), 1)
        key = (col // R_NEW_DEV) * TOK + part * R_NEW_DEV + col % R_NEW_DEV
        bias[...] = jnp.where(key <= token, 0.0, HIDDEN)

    def scores(i, keys):
        return lax.dot_general(qbuf[i], keys, NT, preferred_element_type=f32)

    def step(j, kind):
        if kind in ("diagonal", "first"):
            rows = slice(0, R_CHUNK)
        else:
            rows = pl.ds(pl.multiple_of(j * R_CHUNK, R_CHUNK), R_CHUNK)
        keys = kbuf[rows, :]
        values = vbuf[rows, :]
        before, above = (old_acc, old_top) if kind == "first" else (acc, top)
        if kind == "later":
            at = lax.broadcasted_iota(jnp.int32, (1, R_CHUNK), 1) + j * R_CHUNK
            tail = jnp.where(at < count, 0.0, HIDDEN)
        s_now = scores(0, keys)
        for i in range(R_UNITS):
            ahead = scores(i + 1, keys) if i + 1 < R_UNITS else None
            if kind == "diagonal":
                s_now = jnp.concatenate([s_now[:, 0:R_NEW] + bias[...], s_now[:, R_NEW:]], 1)
            if kind == "later":
                s_now = s_now + tail
            fresh = jnp.broadcast_to(jnp.max(s_now, -1, keepdims=True), (R_QUERIES, DH))
            if kind != "diagonal":
                old = above[i]
                fresh = jnp.maximum(old, fresh)
                shrink = jnp.exp2((old - fresh) * LOG2E_SCALED)
            shift = jnp.concatenate([fresh * LOG2E_SCALED] * (R_CHUNK // DH), 1)
            p = jnp.exp2(s_now * LOG2E_SCALED - shift).astype(bf16)
            d = jnp.dot(p, values, preferred_element_type=f32)
            if kind != "diagonal":
                d = before[i] * jnp.concatenate([shrink, shrink], 1) + d
            top[i] = fresh
            acc[i] = d
            s_now = ahead

    def later_step(j, _):
        step(j, "later")
        return 0

    for copy in at_once:
        copy.wait()
    step(0, "diagonal" if phase == 0 else "first")
    for seen, copies in later:

        @pl.when(seen)
        def _():
            for copy in copies:
                copy.wait()

    lax.fori_loop(1, (count + R_CHUNK - 1) // R_CHUNK, later_step, 0)

    if phase < 2:
        return

    lane = lax.broadcasted_iota(jnp.int32, (PIECE, DH), 1)
    logs = jnp.zeros((PIECE, DH), f32)
    copies = []

    def give(i):
        cols = slice(i * DH, (i + 1) * DH)
        copies.append(pltpu.make_async_copy(obuf.at[:, :, cols], out.at[:, :, cols], out_sems.at[i]))
        copies[-1].start()

    for i in range(GROUP):
        rows = slice((i % 2) * PIECE, (i % 2 + 1) * PIECE)
        total = acc[i // 2, rows, DH:]
        o = (acc[i // 2, rows, 0:DH] / total).astype(bf16)
        obuf[:, :, i * DH : (i + 1) * DH] = o.reshape(RING, TOK, DH)
        give(i)
        log = top[i // 2, rows] * LOG2E_SCALED + jnp.log2(total)
        hi = log.astype(bf16).astype(f32)
        mid = (log - hi).astype(bf16).astype(f32)
        lo = log - hi - mid
        logs = jnp.where(lane == 3 * i, hi, logs)
        logs = jnp.where(lane == 3 * i + 1, mid, logs)
        logs = jnp.where(lane == 3 * i + 2, lo, logs)
    obuf[:, :, WIDE:] = logs.astype(bf16).reshape(RING, TOK, DH)
    give(GROUP)
    for copy in copies:
        copy.wait()


def place_passing_kernel(flags, passing, _, out, sems):
    def copy(g):
        return pltpu.make_async_copy(passing.at[g], out.at[:, g * WIDE : (g + 1) * WIDE], sems.at[g])

    for g in range(KVH):

        @pl.when(flags[g] == 0)
        def _():
            copy(g).start()

    for g in range(KVH):

        @pl.when(flags[g] == 0)
        def _():
            copy(g).wait()


def merge_kernel(flags, partial, out, wide, sems):
    groups = retrieval_groups(flags)
    copies = []
    for which in range(2):
        pieces = [partial[which * KEY_PARTS + kp] for kp in range(KEY_PARTS)]
        logs3 = [piece[:, WIDE:].astype(f32) for piece in pieces]
        for i in range(GROUP):
            logs = [
                l[:, 3 * i : 3 * i + 1] + l[:, 3 * i + 1 : 3 * i + 2] + l[:, 3 * i + 2 : 3 * i + 3] for l in logs3
            ]
            top = functools.reduce(jnp.maximum, logs)
            shares = [jnp.exp2(x - top) for x in logs]
            total = functools.reduce(jnp.add, shares)
            o = sum(
                piece[:, i * DH : (i + 1) * DH].astype(f32) * (share / total)
                for piece, share in zip(pieces, shares)
            )
            wide[which, :, i * DH : (i + 1) * DH] = o.astype(bf16)
        columns = pl.ds(pl.multiple_of(groups[which] * WIDE, WIDE), WIDE)
        copies.append(pltpu.make_async_copy(wide.at[which], out.at[:, columns], sems.at[which]))
        copies[-1].start()
    for copy in copies:
        copy.wait()


def swap(x, axis):
    return lax.all_to_all(x, axis, split_axis=0, concat_axis=0, tiled=True)


def body(queries, new_keys, new_values, cache_keys, cache_values, retrieval, sinks, windows):
    column_index = lax.axis_index("zl") * RING + lax.axis_index("x")
    place = jnp.stack([lax.axis_index("seq"), column_index]).astype(jnp.int32)

    def send(x, pairs):
        return lax.ppermute(x, "seq", pairs)

    sds = jax.ShapeDtypeStruct
    two = 2 * DH
    packed, cache = call(
        pack_kv_kernel,
        (sds((HEAD, TOK + R_SEND, two), bf16), sds((PRE, two), bf16)),
        (retrieval, new_keys, new_values, cache_keys, cache_values),
        vmem=60,
    )
    got = swap(packed, ("zl", "x"))
    first = send(cache, [(10, 13), (12, 14), (14, 15), (0, 8)])
    second = send(cache, [(11, 13), (13, 14), (0, 4)])
    third = send(cache, [(0, 12)])
    ring = sds((TOK, WIDE), bf16)
    packed_q, *rings = call(
        pack_q_kernel,
        (sds((HEAD, TOK, WIDE), bf16), ring, ring, ring, ring),
        (retrieval, place, queries),
    )
    got, first, second, third, packed_q, *rings = lax.optimization_barrier(
        (got, first, second, third, packed_q, *rings)
    )
    rows = sds((CARRY, two), bf16)
    part, own, two_on, odd_on = call(
        unpack_kv_kernel,
        (sds((R_ROWS, two), bf16), rows, rows, rows),
        (retrieval, place, got, cache, first, second, third),
    )
    cells = [(y, zh, c) for y in range(4) for zh in range(2) for c in range(2)]
    part, *rings = lax.optimization_barrier((part, *rings))
    back_z = send(part, [(4 * y + 2 * z + c, 4 * y + 2 * (1 - z) + c) for y, z, c in cells])
    rings = rings[:1] + [
        lax.ppermute(rings[k], "x", [(i, (i + k) % RING) for i in range(RING)]) for k in (1, 2, 3)
    ]
    column = jnp.concatenate([part, back_z], 0)
    column, packed_q = lax.optimization_barrier((column, packed_q))
    q = swap(packed_q, ("zl", "x"))
    own_core = [column] + [send(column, [(i, (i + 4 * k) % SEQ) for i in range(SEQ)]) for k in (1, 2, 3)]
    def other_core(x):
        return send(x, [(i, i ^ 1) for i in range(SEQ)])

    across = other_core(column)
    state = (
        sds((R_UNITS, R_QUERIES, 2 * DH), f32),
        sds((R_UNITS, R_QUERIES, DH), f32),
        sds((R_UNITS, R_QUERIES, DH), bf16),
    )
    dma = pltpu.SemaphoreType.DMA
    buffers = [
        pltpu.VMEM((R_KEYS, DH), bf16),
        pltpu.VMEM((R_KEYS, 2 * DH), bf16),
        dma((24,)),
    ]
    flops = R_UNITS * R_QUERIES * R_KEYS * 4 * DH
    acc, top, queried = call(
        functools.partial(retrieval_kernel, 0),
        state,
        (place, *rings, column, across),
        flops=flops,
        nbytes=2**22,
        scratch=buffers + [pltpu.VMEM((R_QUERIES, R_NEW), f32), dma((RING * GROUP,))],
        vmem=24,
        by_hand=True,
        resident=state,
    )
    same = own_core[1:]
    acc, two_on, odd_on, *same = lax.optimization_barrier((acc, two_on, odd_on, *same))
    other = [other_core(x) for x in same]
    back_two = send(two_on, [(i, (i + 2) % SEQ) for i in range(SEQ)])
    near = send(odd_on, [(i, (i + 1 + 2 * (i % 2)) % SEQ) for i in range(SEQ)])
    acc, top = call(
        functools.partial(retrieval_kernel, 1),
        state[:2],
        (place, *same, queried, acc, top),
        flops=flops,
        nbytes=2**22,
        scratch=buffers,
        vmem=24,
        by_hand=True,
        resident=(*state, queried, acc, top),
    )
    acc, top, back_two, *other = lax.optimization_barrier((acc, top, back_two, *other))
    far = other_core(back_two)
    partial = call(
        functools.partial(retrieval_kernel, 2),
        sds((RING, TOK, R_LANES), bf16),
        (place, *other, queried, acc, top),
        flops=flops,
        nbytes=2**22,
        scratch=buffers
        + [pltpu.VMEM(a.shape, f32) for a in state[:2]]
        + [pltpu.VMEM((RING, TOK, R_LANES), bf16), dma((GROUP + 1,))],
        vmem=24,
        by_hand=True,
        resident=(queried, acc, top),
    )
    partial, q, far, near, back_two = lax.optimization_barrier((partial, q, far, near, back_two))
    partial_back = swap(partial, "x")
    passing = call(
        passing_kernel,
        sds((HEAD, TOK, WIDE), bf16),
        (place, retrieval, sinks, windows, q, far, back_two, near, own),
        flops=BLOCK * GROUP * P_KEYS * 4 * DH,
        nbytes=2**22,
        scratch=[
            pltpu.VMEM((4 * BLOCK, DH), bf16),
            pltpu.VMEM((4 * BLOCK, DH), bf16),
            pltpu.VMEM((P_KEYS, DH), bf16),
            pltpu.VMEM((P_KEYS, 2 * DH), bf16),
            pltpu.VMEM((HEAD, TOK, WIDE), bf16),
            pltpu.VMEM((HEAD, TOK, WIDE), bf16),
            pltpu.VMEM((P_TILE, P_KEYS), f32),
            dma((10,)),
            dma((GROUP,)),
            dma((BLOCK // P_TILE, GROUP)),
        ],
        vmem=58,
        by_hand=True,
    )
    passing, partial_back = lax.optimization_barrier((passing, partial_back))
    passing_back = swap(passing, ("zl", "x"))
    anywhere = pl.BlockSpec(memory_space=pl.ANY)
    result = sds((TOK, HQ * DH), bf16)
    merged = pl.pallas_call(
        merge_kernel,
        out_shape=result,
        in_specs=[SMEM, VMEM],
        out_specs=anywhere,
        scratch_shapes=[pltpu.VMEM((2, TOK, WIDE), bf16), pltpu.SemaphoreType.DMA((2,))],
        compiler_params=pltpu.CompilerParams(vmem_limit_bytes=44 * 2**20),
    )(retrieval, partial_back)
    return pl.pallas_call(
        place_passing_kernel,
        out_shape=result,
        in_specs=[SMEM, anywhere, anywhere],
        out_specs=anywhere,
        input_output_aliases={2: 0},
        scratch_shapes=[pltpu.SemaphoreType.DMA((KVH,))],
        compiler_params=pltpu.CompilerParams(vmem_limit_bytes=44 * 2**20),
    )(retrieval, passing_back, merged)


def solution(mesh):
    cut = jax.sharding.Mesh(mesh.devices.reshape(SEQ, 2, RING), ("seq", "zl", "x"))
    tokens = P(("seq", "zl", "x"), None)
    cache = P("seq", ("zl", "x"))
    return jax.shard_map(
        body,
        mesh=cut,
        in_specs=(tokens, tokens, tokens, cache, cache, P(), P(), P()),
        out_specs=tokens,
        check_vma=False,
    )
```
